32 devices in a mesh: blk: 16 (over z, y, core), rep: 2 (over x).
Axes of the slice: x: 2, y: 2, z: 4, core: 2. Of those that a mesh axis runs over, the one named last changes fastest.
Arguments:
- features: bfloat16 [8192, 128], P('blk'), may hold values from -6 to 6
- weight: bfloat16 [128, 256], replicated, may hold values from -0.5 to 0.5
- tile_vals: bfloat16 [16, 2, 8, 12, 128, 128], P('blk', 'rep'), may hold values from -0.078125 to 0.078125
- tile_pos: int32 [16, 2, 8, 12], P('blk', 'rep'), may hold values from 0 to 15, as said below
- tile_count: int32 [16, 2, 8], P('blk', 'rep'), may hold values from 1 to 12, as said below
- cotangent: bfloat16 [8192, 256], P(('blk', 'rep')), may hold values from -6 to 6
Outputs:
- activations: bfloat16 [8192, 256], P(('blk', 'rep'))
- feat_grad: bfloat16 [8192, 128], P(('blk', 'rep'))
- weight_grad: float32 [128, 256], replicated
The draws below stay inside these ranges and needn't reach their ends.
Inputs may be any that keep to these rules, and one draw needn't show every extreme that they name: `tile_pos`: within one row group, copy and section the entries are distinct. `tile_count`: row group 0 has all 12 slots live in every copy and section.
All inputs are finite; a program needn't handle non-finite values.
Results may differ from the reference program's by a relative error of at most 0.014.
Values may be sent and summed in bfloat16 or wider, within the bound.
No kernel may reach another device: no remote copies, remote signals or barrier semaphores. Data moves between devices by JAX's collectives and lax.ppermute only.
A program may use at most 128 MiB of HBM per device.

```python
import jax
import jax.numpy as jnp
from jax import lax

FEAT = 128
HID = 256
TILE = 128
NB_DEV = 4
TILES = 12
SECTIONS = 8
NODES = 8192
N_BLK = 16
N_REP = 2


def draw_tile_pos(key, part):
    cells = NB_DEV * NB_DEV
    scores = jax.random.randint(key, (N_BLK, N_REP, SECTIONS, cells), 0, 1 << 20) * cells
    scores = scores + jnp.arange(cells, dtype=jnp.int32)
    ordering = jnp.argsort(scores, axis=-1, stable=True)
    return ordering[..., :TILES].astype(jnp.int32)


def draw_tile_count(key, part):
    base_count = jax.random.randint(jax.random.fold_in(key, 1), (N_BLK, N_REP, SECTIONS), 1, TILES // 2 + 1)
    group_extra = jax.random.randint(jax.random.fold_in(key, 2), (N_BLK, 1, 1), 0, TILES // 2 + 1)
    counted = jnp.minimum(base_count + group_extra, TILES)
    counted = counted.at[0].set(TILES)
    return counted.astype(jnp.int32)


def level_of(own_key, shape, shards, least, largest):
    loudness, own = 1.0, jax.random.fold_in(own_key, 6)
    for axis_at, shards_of in shards:
        heights = jnp.exp(jax.random.uniform(jax.random.fold_in(own, axis_at), (shards_of,), jnp.float32, least / len(shards), largest / len(shards)))
        loudness = loudness * jnp.repeat(heights, shape[axis_at] // shards_of).reshape([-1 if axis == axis_at else 1 for axis in range(len(shape))])
    return loudness


def normal_values(key, extent, spread, bound, pieces=(), kind=jnp.bfloat16):
    result = jax.random.normal(key, extent, jnp.float32) * spread
    if len(pieces) > 0:
        result = level_of(key, extent, pieces, -0.22, 0.18) * result
    return jnp.clip(result, min=-bound, max=bound).astype(kind)


def setup_inputs(seed: int = 0) -> dict:
    streams_of = jax.random.split(jax.random.key(seed), 7)
    return {
        "features": normal_values(streams_of[0], (NODES, FEAT), 1.0, 6.0, ((0, 16),)),
        "weight": normal_values(streams_of[1], (FEAT, HID), FEAT ** -0.5, 0.5),
        "tile_vals": normal_values(streams_of[2], (N_BLK, N_REP, SECTIONS, TILES, TILE, TILE), (N_BLK * TILES * TILE // NB_DEV) ** -0.5, 0.078125, ((0, 16), (1, 2))),
        "tile_pos": draw_tile_pos(jax.random.fold_in(streams_of[6], 71), 0),
        "tile_count": draw_tile_count(jax.random.fold_in(streams_of[6], 71), 0),
        "cotangent": normal_values(streams_of[5], (NODES, HID), 1.0, 6.0, ((0, 32),)),
    }


def gelu_tanh(value):
    return jax.nn.gelu(value, approximate=True)

def reference(features, weight, tile_vals, tile_pos, tile_count, cotangent):
    section_count = N_BLK // N_REP
    hidden = jnp.dot(features, weight, preferred_element_type=jnp.float32).astype(jnp.bfloat16)
    hidden_blocks = hidden.reshape(N_BLK * NB_DEV, TILE, HID)
    rep_ids = jnp.arange(N_REP, dtype=jnp.int32)[:, None]
    section_ids = jnp.arange(section_count, dtype=jnp.int32)[None, :]
    offsets = rep_ids + section_ids * N_REP
    live_mask = (jnp.arange(TILES, dtype=jnp.int32)[None, None, None, :] < tile_count[..., None]).astype(jnp.float32)
    block_ids = jnp.arange(NB_DEV, dtype=jnp.int32)

    def forward_group(group):
        columns = (group - offsets) % N_BLK
        positions = tile_pos[group]
        col_index = columns[..., None] * NB_DEV + positions % NB_DEV
        picked = hidden_blocks[col_index].astype(jnp.float32)
        tile_block = tile_vals[group].astype(jnp.float32) * live_mask[group][..., None, None]
        product = jnp.einsum('rstik,rstkf->rstif', tile_block, picked)
        placing = ((positions // NB_DEV)[..., None] == block_ids).astype(jnp.float32)
        return jnp.einsum('rstn,rstif->nif', placing, product).reshape(NB_DEV * TILE, HID)
    pre = lax.map(forward_group, jnp.arange(N_BLK, dtype=jnp.int32)).reshape(NODES, HID)
    outputs, pullback = jax.vjp(gelu_tanh, pre)
    activations = outputs.astype(jnp.bfloat16)
    pre_grad = pullback(cotangent.astype(jnp.float32))[0].astype(jnp.bfloat16)
    grad_blocks = pre_grad.reshape(N_BLK * NB_DEV, TILE, HID)
    rep_grid = jnp.broadcast_to(rep_ids, (N_REP, section_count))
    section_grid = jnp.broadcast_to(section_ids, (N_REP, section_count))

    def backward_group(column):
        sources = (column + offsets) % N_BLK
        positions = tile_pos[sources, rep_grid, section_grid]
        tile_block = tile_vals[sources, rep_grid, section_grid].astype(jnp.float32)
        tile_block = tile_block * live_mask[sources, rep_grid, section_grid][..., None, None]
        row_index = sources[..., None] * NB_DEV + positions // NB_DEV
        picked = grad_blocks[row_index].astype(jnp.float32)
        product = jnp.einsum('rstki,rstkf->rstif', tile_block, picked)
        placing = ((positions % NB_DEV)[..., None] == block_ids).astype(jnp.float32)
        return jnp.einsum('rstn,rstif->nif', placing, product).reshape(NB_DEV * TILE, HID)
    hidden_grad = lax.map(backward_group, jnp.arange(N_BLK, dtype=jnp.int32)).reshape(NODES, HID)
    hidden_grad = hidden_grad.astype(jnp.bfloat16)
    weight_grad = jnp.dot(features.T, hidden_grad, preferred_element_type=jnp.float32)
    feat_grad = jnp.dot(hidden_grad, weight.T, preferred_element_type=jnp.float32).astype(jnp.bfloat16)
    return (activations, feat_grad, weight_grad)
```

```python
import functools

import jax
import jax.numpy as jnp
from jax import lax
from jax.experimental import pallas as pl
from jax.experimental.pallas import tpu as pltpu
from jax.sharding import PartitionSpec as P

AXES = ("blk", "rep")
VMEM_LIMIT = 32 * 1024 * 1024


def params():
    return pltpu.CompilerParams(vmem_limit_bytes=VMEM_LIMIT)


def in_vmem(count):
    return [pl.BlockSpec(memory_space=pltpu.VMEM)] * count


def gelu_and_slope(v):
    scale = 0.7978845608028654
    square = v * v
    t = jnp.tanh(scale * (v + 0.044715 * (square * v)))
    half = 0.5 * (1.0 + t)
    slope = half + (0.5 * scale) * v * (1.0 - t * t) * (1.0 + 3.0 * 0.044715 * square)
    return v * half, slope


def nt_dot(a, b):
    return lax.dot_general(a, b, (((1,), (1,)), ((), ())), preferred_element_type=jnp.float32)


def tn_dot(a, b):
    return lax.dot_general(a, b, (((0,), (0,)), ((), ())), preferred_element_type=jnp.float32)


def dot(a, b):
    return jnp.dot(a, b, preferred_element_type=jnp.float32)


def dense_kernel(blocks, halves, pos, count, place, flip, tiles_ref, out_ref):
    section = pl.program_id(0)
    tile = tiles_ref.shape[-1]
    per_half = blocks // halves
    out_ref[...] = jnp.zeros_like(out_ref)
    for slot in range(tiles_ref.shape[1]):
        position = pos[section, slot]
        row = lax.div(position, blocks) ^ flip[0]
        col = lax.rem(position, blocks) ^ flip[0]
        half = lax.div(col, per_half)
        row_at = pl.multiple_of(row * tile, tile)
        col_at = pl.multiple_of(lax.rem(col, per_half) * tile, tile)

        @pl.when(slot < count[section])
        def _():
            out_ref[0, half, pl.ds(row_at, tile), pl.ds(col_at, tile)] = tiles_ref[0, slot]


def dense_blocks(tiles, pos, count, place, flip, near, halves, blocks):
    sections, slots, tile = tiles.shape[0], tiles.shape[1], tiles.shape[-1]
    rows = blocks * tile
    piece = rows // halves
    grid_spec = pltpu.PrefetchScalarGridSpec(
        num_scalar_prefetch=4,
        grid=(sections,),
        in_specs=[pl.BlockSpec((1, slots, tile, tile), lambda j, *_: (j, 0, 0, 0))],
        out_specs=pl.BlockSpec(
            (1, halves, rows, piece),
            lambda j, pos, count, place, flip: (lax.rem(place[j], near), 0, 0, lax.div(place[j], near)),
        ),
    )
    return pl.pallas_call(
        functools.partial(dense_kernel, blocks, halves),
        grid_spec=grid_spec,
        out_shape=jax.ShapeDtypeStruct((near, halves, rows, sections // near * piece), jnp.bfloat16),
        compiler_params=params(),
        name="dense_blocks",
    )(pos, count, place, flip, tiles)


def aggregate_kernel(dense_ref, *refs):
    parts, (total_ref, sent_ref) = refs[:-2], refs[-2:]
    halves = dense_ref.shape[1]
    total = None
    for at, part in enumerate(parts):
        term = dot(dense_ref[at // halves, at % halves], part[...])
        total = term if total is None else total + term
    total_ref[...] = total
    sent_ref[...] = total.astype(jnp.bfloat16)


def aggregate(dense, parts):
    rows, width = dense.shape[2], parts[0].shape[1]
    return pl.pallas_call(
        aggregate_kernel,
        in_specs=in_vmem(1 + len(parts)),
        out_specs=in_vmem(2),
        out_shape=[
            jax.ShapeDtypeStruct((rows, width), jnp.float32),
            jax.ShapeDtypeStruct((rows, width), jnp.bfloat16),
        ],
        compiler_params=params(),
        name="aggregate",
    )(dense, *parts)


def turn_kernel(share, own_ref, other_ref, weight_ref, cot_ref, far_cot_ref, dense_ref,
                act_ref, g_ref, grad_ref, back_ref, *sent_refs):
    rows = own_ref.shape[0]
    weight = weight_ref[...]
    for half, cot in enumerate((cot_ref, far_cot_ref)):
        at, there = half * share, rows - share - half * share
        g = (own_ref[pl.ds(at, share)] + other_ref[pl.ds(there, share)].astype(jnp.float32)).astype(jnp.bfloat16)
        value, slope = gelu_and_slope(dot(g, weight))
        grad = (cot[...].astype(jnp.float32) * slope).astype(jnp.bfloat16)
        if half == 0:
            act_ref[...] = value.astype(jnp.bfloat16)
            g_ref[...] = g
            grad_ref[...] = grad
        back_ref[:, pl.ds(at, share)] = nt_dot(weight, grad).astype(jnp.bfloat16)
    back = back_ref[...]
    halves = dense_ref.shape[1]
    for at, sent in enumerate(sent_refs, 1):
        sent[...] = dot(back, dense_ref[at // halves, at % halves]).astype(jnp.bfloat16)


def turn(own, other, weight, cot, far_cot, dense):
    rows, width = own.shape
    share, hid = cot.shape
    near, halves, _, span = dense.shape
    bf = jnp.bfloat16
    return pl.pallas_call(
        functools.partial(turn_kernel, share),
        in_specs=in_vmem(6),
        out_specs=in_vmem(4 + near * halves - 1),
        out_shape=[
            jax.ShapeDtypeStruct((share, hid), bf),
            jax.ShapeDtypeStruct((share, width), bf),
            jax.ShapeDtypeStruct((share, hid), bf),
            jax.ShapeDtypeStruct((width, rows), bf),
        ] + [jax.ShapeDtypeStruct((width, span), bf)] * (near * halves - 1),
        compiler_params=params(),
        name="turn",
    )(own, other, weight, cot, far_cot, dense)


def kept_kernel(back_ref, dense_ref, g_ref, grad_ref, kept_ref, wg_ref):
    wg_ref[...] = tn_dot(g_ref[...], grad_ref[...])
    kept_ref[...] = dot(back_ref[...], dense_ref[0, 0])


def kept_terms(back, dense, g, grad):
    width, span, hid = back.shape[0], dense.shape[3], grad.shape[1]
    return pl.pallas_call(
        kept_kernel,
        in_specs=in_vmem(4),
        out_specs=in_vmem(2),
        out_shape=[
            jax.ShapeDtypeStruct((width, span), jnp.float32),
            jax.ShapeDtypeStruct((width, hid), jnp.float32),
        ],
        compiler_params=params(),
        name="kept_terms",
    )(back, dense, g, grad)


def near_sum_kernel(kept_ref, a_ref, b_ref, c_ref, wg_ref, *out_refs):
    width = kept_ref.shape[0]
    piece = kept_ref.shape[1] // len(out_refs)
    wg = wg_ref[...].astype(jnp.bfloat16)
    for at, out in enumerate(out_refs):
        span = pl.ds(at * piece, piece)
        total = kept_ref[:, span] + a_ref[:, span].astype(jnp.float32)
        total += b_ref[:, span].astype(jnp.float32) + c_ref[:, span].astype(jnp.float32)
        out[0:width, :] = total.astype(jnp.bfloat16)
        out[width:, :] = wg


def near_sum(kept, parts, wg, far):
    width, span = kept.shape
    return pl.pallas_call(
        near_sum_kernel,
        in_specs=in_vmem(5),
        out_specs=in_vmem(far),
        out_shape=[jax.ShapeDtypeStruct((width + wg.shape[0], span // far), jnp.bfloat16)] * far,
        compiler_params=params(),
        name="near_sum",
    )(kept, *parts, wg)


def far_sum_kernel(*refs):
    parts, (feat_ref, wg_ref) = refs[:-2], refs[-2:]
    width = feat_ref.shape[1]
    terms = [part[...].astype(jnp.float32) for part in parts]
    while len(terms) > 1:
        terms = [terms[i] + terms[i + 1] for i in range(0, len(terms), 2)]
    feat_ref[...] = terms[0][0:width].T.astype(jnp.bfloat16)
    wg_ref[...] = terms[0][width:]


def far_sum(parts, width):
    total, piece = parts[0].shape
    return pl.pallas_call(
        far_sum_kernel,
        in_specs=in_vmem(len(parts)),
        out_specs=in_vmem(2),
        out_shape=[
            jax.ShapeDtypeStruct((piece, width), jnp.bfloat16),
            jax.ShapeDtypeStruct((total - width, piece), jnp.float32),
        ],
        compiler_params=params(),
        name="far_sum",
    )(*parts)


class Layout:
    def __init__(self, n_blk, reps):
        self.n_blk, self.reps = n_blk, reps

    def route(self, moved):
        pairs = []
        for b in range(self.n_blk):
            for r in range(self.reps):
                to_b, to_r = moved(b, r)
                pairs.append((b * self.reps + r, to_b * self.reps + to_r))
        return pairs

    def owner_to_class(self, mask):
        reps = self.reps
        return self.route(lambda b, r: (((b // reps) ^ mask) * reps + (b + r) % reps, r))

    def class_to_owner(self, mask):
        reps = self.reps
        return self.route(lambda b, r: (((b // reps) ^ mask) * reps + (b - r) % reps, r))

    def in_class(self, mask, rep_mask):
        reps = self.reps

        def moved(b, r):
            to_r = r ^ rep_mask
            return (((b // reps) ^ mask) * reps + (b - r + to_r) % reps, to_r)

        return self.route(moved)

    def plain(self, mask, rep_mask):
        return self.route(lambda b, r: (b ^ mask, r ^ rep_mask))


def send(value, route):
    return lax.ppermute(value, AXES, route)


def section_places(sections):
    reps, n_blk = lax.axis_size("rep"), lax.axis_size("blk")
    b, r = lax.axis_index("blk"), lax.axis_index("rep")
    columns = (b - r - jnp.arange(sections, dtype=jnp.int32) * reps) % n_blk
    return (columns // reps) ^ (b // reps)


def local_pairs(features, weight, tiles, pos, count, cotangent):
    near, halves = 2, 2
    lay = Layout(lax.axis_size("blk"), lax.axis_size("rep"))
    b, r = lax.axis_index("blk"), lax.axis_index("rep")
    sections, tile = tiles.shape[0], tiles.shape[-1]
    rows, width = features.shape
    blocks, share, far = rows // tile, rows // halves, sections // near
    flip = (r * (blocks // halves)).astype(jnp.int32).reshape(1)
    quad = ((0, 1), (1, 0), (1, 1))

    own_rows = lax.dynamic_slice_in_dim(features, r * share, share, 0)
    line = jnp.concatenate([send(own_rows, lay.owner_to_class(at * near)) for at in range(far)], 0)
    far_cot = send(cotangent, lay.plain(0, 1))
    parts = [line] + [send(line, lay.in_class(*mask)) for mask in quad]
    dense = dense_blocks(tiles, pos, count, section_places(sections), flip, near, halves, blocks)
    partial, sent = aggregate(dense, parts)
    other = send(sent, lay.plain(0, 1))
    act, g, grad, back, *outgoing = turn(partial, other, weight, cotangent, far_cot, dense)
    arrived = [send(value, lay.in_class(*mask)) for value, mask in zip(outgoing, quad)]
    kept, wg = kept_terms(back, dense, g, grad)

    lane = b % 2
    wg_rows = wg.shape[0] // 2
    wg_own = lax.dynamic_slice_in_dim(wg, lane * wg_rows, wg_rows, 0)
    wg_sent = lax.dynamic_slice_in_dim(wg, (1 - lane) * wg_rows, wg_rows, 0)
    wg_own = wg_own + send(wg_sent, lay.plain(1, 0))
    wg_own = wg_own + send(wg_own, lay.plain(0, 1))
    wg_own = wg_own + send(wg_own, lay.plain(2, 0))

    lines = near_sum(kept, arrived, wg_own, far)
    lines = [send(value, lay.class_to_owner(at * near)) for at, value in enumerate(lines)]
    feat_grad, wg_half = far_sum(lines, width)
    wg_other = send(wg_half, lay.plain(1, 0))
    first = (lane ^ r) == 0
    weight_grad = jnp.concatenate(
        [jnp.where(first, wg_half, wg_other), jnp.where(first, wg_other, wg_half)], 0
    )
    return act, feat_grad, weight_grad


def local_any(features, weight, tiles, pos, count, cotangent):
    reps = lax.axis_size("rep")
    lay = Layout(lax.axis_size("blk"), reps)
    r = lax.axis_index("rep")
    sections, tile = tiles.shape[0], tiles.shape[-1]
    rows = features.shape[0]
    blocks, share = rows // tile, rows // reps
    bf = jnp.bfloat16

    line = jnp.concatenate([send(features, lay.owner_to_class(at)) for at in range(sections)], 0)
    flip = jnp.zeros((1,), jnp.int32)
    dense = dense_blocks(tiles, pos, count, section_places(sections), flip, 1, 1, blocks)
    partial, _ = aggregate(dense, [line])
    g = lax.psum(partial, "rep").astype(bf)
    value, slope = gelu_and_slope(dot(g, weight))
    cot = lax.all_gather(cotangent, "rep", axis=0, tiled=True)
    grad = (cot.astype(jnp.float32) * slope).astype(bf)
    act = lax.dynamic_slice_in_dim(value, r * share, share, 0).astype(bf)
    own_g = lax.dynamic_slice_in_dim(g, r * share, share, 0)
    own_grad = lax.dynamic_slice_in_dim(grad, r * share, share, 0)
    weight_grad = lax.psum(tn_dot(own_g, own_grad), AXES)
    back = nt_dot(weight, grad).astype(bf)
    terms = dot(back, dense[0, 0]).astype(bf)
    total = jnp.zeros((back.shape[0], rows), jnp.float32)
    for at in range(sections):
        total += send(terms[:, at * rows:(at + 1) * rows], lay.class_to_owner(at)).astype(jnp.float32)
    feat_grad = lax.psum_scatter(total.T, "rep", scatter_dimension=0, tiled=True).astype(bf)
    return act, feat_grad, weight_grad


def local(features, weight, tile_vals, tile_pos, tile_count, cotangent):
    tiles, pos, count = tile_vals[0, 0], tile_pos[0, 0], tile_count[0, 0]
    reps, tile = lax.axis_size("rep"), tiles.shape[-1]
    paired = reps == 2 and tiles.shape[0] == 8 and features.shape[0] % (2 * tile) == 0
    work = local_pairs if paired else local_any
    return work(features, weight, tiles, pos, count, cotangent)


def solution(mesh):
    placed = (
        P("blk", None),
        P(),
        P("blk", "rep", None, None, None, None),
        P("blk", "rep", None, None),
        P("blk", "rep", None),
        P(("blk", "rep"), None),
    )
    return jax.shard_map(
        local,
        mesh=mesh,
        in_specs=placed,
        out_specs=(P(("blk", "rep"), None), P(("blk", "rep"), None), P()),
        check_vma=False,
    )
```

```python
import functools

import jax
import jax.numpy as jnp
from jax import lax
from jax.experimental import pallas as pl
from jax.experimental.pallas import tpu as pltpu
from jax.sharding import PartitionSpec as P

AXES = ("blk", "rep")
VMEM_LIMIT = 16 * 1024 * 1024


def params():
    return pltpu.CompilerParams(vmem_limit_bytes=VMEM_LIMIT)


def in_vmem(count):
    return [pl.BlockSpec(memory_space=pltpu.VMEM)] * count


def held_in_vmem(value):
    return pltpu.with_memory_space_constraint(value, pltpu.VMEM)


def gelu_and_slope(v):
    scale = 0.7978845608028654
    square = v * v
    t = jnp.tanh(scale * (v + 0.044715 * (square * v)))
    half = 0.5 * (1.0 + t)
    slope = half + (0.5 * scale) * v * (1.0 - t * t) * (1.0 + 3.0 * 0.044715 * square)
    return v * half, slope


def nt_dot(a, b):
    return lax.dot_general(a, b, (((1,), (1,)), ((), ())), preferred_element_type=jnp.float32)


def tn_dot(a, b):
    return lax.dot_general(a, b, (((0,), (0,)), ((), ())), preferred_element_type=jnp.float32)


def dot(a, b):
    return jnp.dot(a, b, preferred_element_type=jnp.float32)


def dense_kernel(blocks, near, halves, table, tiles_ref, out_ref, done_ref, held, arrived):
    sections, slots, tile = held.shape[0], held.shape[1], held.shape[-1]
    piece = out_ref.shape[2] // (sections // near)
    per_half = blocks // halves
    copies = [
        pltpu.make_async_copy(tiles_ref.at[section], held.at[section], arrived.at[section])
        for section in range(sections)
    ]
    for copy in copies:
        copy.start()
    out_ref[...] = jnp.zeros_like(out_ref)
    done_ref[...] = jnp.zeros_like(done_ref)
    for section, copy in enumerate(copies):
        copy.wait()
        place = table[section, slots]
        unit = lax.rem(place, near) * halves
        base = lax.div(place, near) * piece
        for slot in range(slots):
            cell = table[section, slot]
            row_at = pl.multiple_of(lax.div(cell, blocks) * tile, tile)
            col = lax.rem(cell, blocks)
            col_at = pl.multiple_of(base + lax.rem(col, per_half) * tile, tile)
            half = lax.div(col, per_half)

            @pl.when(cell >= 0)
            def _():
                out_ref[unit + half, pl.ds(row_at, tile), pl.ds(col_at, tile)] = held[section, slot]


def dense_blocks(tiles, table, near, halves, blocks):
    sections, _, tile, _ = tiles.shape
    rows = blocks * tile
    shape = (near * halves, rows, sections // near * rows // halves)
    return pl.pallas_call(
        functools.partial(dense_kernel, blocks, near, halves),
        in_specs=[pl.BlockSpec(memory_space=pltpu.SMEM), pl.BlockSpec(memory_space=pltpu.HBM)],
        out_specs=in_vmem(2),
        out_shape=[pltpu.VMEM(shape, jnp.bfloat16), jax.ShapeDtypeStruct((8, 128), jnp.float32)],
        scratch_shapes=[pltpu.VMEM(tiles.shape, tiles.dtype), pltpu.SemaphoreType.DMA((sections,))],
        compiler_params=params(),
        name="dense_blocks",
    )(table, pltpu.with_memory_space_constraint(tiles, pltpu.HBM))


def unit_at(unit):
    if unit in (0, 3):
        return unit
    lane = lax.rem(lax.axis_index("blk") + lax.axis_index("rep"), 2)
    return 2 - lane if unit == 1 else 1 + lane


def aggregate_kernel(spans, based, dense_ref, *refs):
    given, out_ref = refs[:-1], refs[-1]
    total = given[0][...] if based else None
    for (unit, start, row, size), part in zip(spans, given[based:]):
        term = dot(dense_ref[unit_at(unit), :, pl.ds(start, size)], part[pl.ds(row, size), :])
        total = term if total is None else total + term
    out_ref[...] = total.astype(out_ref.dtype)


def aggregate(dense, spans, parts, base, dtype):
    rows, width = dense.shape[1], parts[0].shape[1]
    given = ([] if base is None else [base]) + parts
    return pl.pallas_call(
        functools.partial(aggregate_kernel, spans, len(given) - len(parts)),
        in_specs=in_vmem(1 + len(given)),
        out_specs=in_vmem(1)[0],
        out_shape=jax.ShapeDtypeStruct((rows, width), dtype),
        compiler_params=params(),
        name="aggregate",
    )(held_in_vmem(dense), *given)


def turn_kernel(share, own_ref, other_ref, weight_ref, cot_ref, far_cot_ref, dense_ref,
                act_ref, back_ref, sent_ref):
    rows = own_ref.shape[0]
    span = dense_ref.shape[2]
    weight = weight_ref[...]
    weight_grad = None
    for half, cot in enumerate((cot_ref, far_cot_ref)):
        at, there = half * share, rows - share - half * share
        g = own_ref[pl.ds(at, share), :].astype(jnp.float32) + other_ref[pl.ds(there, share), :].astype(jnp.float32)
        g = g.astype(jnp.bfloat16)
        value, slope = gelu_and_slope(dot(g, weight))
        grad = (cot[...].astype(jnp.float32) * slope).astype(jnp.bfloat16)
        if half == 0:
            act_ref[...] = value.astype(jnp.bfloat16)
        term = tn_dot(g, grad)
        weight_grad = term if weight_grad is None else weight_grad + term
        back_ref[:, pl.ds(at, share)] = nt_dot(weight, grad).astype(jnp.bfloat16)
    back = back_ref[...]
    half_span = span // 2
    for second in range(2):
        term = dot(back, dense_ref[unit_at(2 + second), :, pl.ds(half_span, half_span)])
        sent_ref[:, pl.ds(second * half_span, half_span)] = term.astype(jnp.bfloat16)
    sent_ref[:, pl.ds(span, weight.shape[1])] = weight_grad.astype(jnp.bfloat16)


def turn(own, other, weight, cot, far_cot, dense):
    rows, width = own.shape
    share, hid = cot.shape
    span = dense.shape[2]
    bf = jnp.bfloat16
    return pl.pallas_call(
        functools.partial(turn_kernel, share),
        in_specs=in_vmem(6),
        out_specs=in_vmem(3),
        out_shape=[
            jax.ShapeDtypeStruct((share, hid), bf),
            jax.ShapeDtypeStruct((width, rows), bf),
            jax.ShapeDtypeStruct((width, span + hid), bf),
        ],
        compiler_params=params(),
        name="turn",
    )(own, other, weight, cot, far_cot, held_in_vmem(dense))


def rest_kernel(back_ref, dense_ref, sent_ref, kept_ref):
    back = back_ref[...]
    half_span = dense_ref.shape[2] // 2
    for second in range(2):
        term = dot(back, dense_ref[unit_at(2 + second), :, pl.ds(0, half_span)])
        sent_ref[:, pl.ds(second * half_span, half_span)] = term.astype(jnp.bfloat16)
    for second in range(2):
        kept_ref[second] = dot(back, dense_ref[unit_at(second)])


def rest_terms(back, dense):
    width, span = back.shape[0], dense.shape[2]
    return pl.pallas_call(
        rest_kernel,
        in_specs=in_vmem(2),
        out_specs=in_vmem(2),
        out_shape=[
            jax.ShapeDtypeStruct((width, span), jnp.bfloat16),
            jax.ShapeDtypeStruct((2, width, span), jnp.float32),
        ],
        compiler_params=params(),
        name="rest_terms",
    )(back, held_in_vmem(dense))


def first_sum_kernel(start, size, got_ref, kept_ref, own_ref, sent_ref, total_ref):
    extra = sent_ref.shape[1] - size
    total_ref[...] = kept_ref[0, :, pl.ds(start, size)] + got_ref[:, pl.ds(0, size)].astype(jnp.float32)
    passed = kept_ref[1, :, pl.ds(start, size)] + got_ref[:, pl.ds(size, size)].astype(jnp.float32)
    sent_ref[:, pl.ds(0, size)] = passed.astype(jnp.bfloat16)
    if extra:
        ours = own_ref[:, pl.ds(2 * size, extra)].astype(jnp.float32)
        theirs = got_ref[:, pl.ds(2 * size, extra)].astype(jnp.float32)
        sent_ref[:, pl.ds(size, extra)] = (ours + theirs).astype(jnp.bfloat16)


def first_sum(start, got, kept, own):
    width = kept.shape[1]
    size = kept.shape[2] // 2
    extra = got.shape[1] - 2 * size
    return pl.pallas_call(
        functools.partial(first_sum_kernel, start, size),
        in_specs=in_vmem(3),
        out_specs=in_vmem(2),
        out_shape=[
            jax.ShapeDtypeStruct((width, size + extra), jnp.bfloat16),
            jax.ShapeDtypeStruct((width, size), jnp.float32),
        ],
        compiler_params=params(),
        name="first_sum",
    )(got, kept, own)


def add_pieces(got_ref, kept_ref, wg, out_refs):
    width, size = kept_ref.shape
    piece = size // 2
    for at, out in enumerate(out_refs):
        span = pl.ds(at * piece, piece)
        out[0:width, :] = (kept_ref[:, span] + got_ref[:, span].astype(jnp.float32)).astype(jnp.bfloat16)
        out[width:, :] = wg


def second_sum_a_kernel(got_ref, kept_ref, own_ref, two_ref, three_ref, wg_ref):
    size, (part, hid) = kept_ref.shape[1], wg_ref.shape
    lane = lax.rem(lax.axis_index("blk") + lax.axis_index("rep"), 2)
    rows = pl.ds(pl.multiple_of(lane * part, part), part)
    wg = own_ref[rows, pl.ds(size, hid)].astype(jnp.float32) + got_ref[rows, pl.ds(size, hid)].astype(jnp.float32)
    wg_ref[...] = wg.astype(jnp.bfloat16)
    add_pieces(got_ref, kept_ref, wg.astype(jnp.bfloat16), (two_ref, three_ref))


def second_sum_b_kernel(got_ref, kept_ref, wg_ref, zero_ref, one_ref):
    add_pieces(got_ref, kept_ref, wg_ref[...], (zero_ref, one_ref))


def message_shape(kept):
    width, size = kept.shape
    return jax.ShapeDtypeStruct((width + width // 2, size // 2), jnp.bfloat16)


def second_sum_a(got, kept, own):
    width, size = kept.shape
    message = message_shape(kept)
    return pl.pallas_call(
        second_sum_a_kernel,
        in_specs=in_vmem(3),
        out_specs=in_vmem(3),
        out_shape=[message, message, jax.ShapeDtypeStruct((width // 2, got.shape[1] - size), jnp.bfloat16)],
        compiler_params=params(),
        name="second_sum_a",
    )(got, kept, own)


def second_sum_b(got, kept, wg):
    return pl.pallas_call(
        second_sum_b_kernel,
        in_specs=in_vmem(3),
        out_specs=in_vmem(2),
        out_shape=[message_shape(kept)] * 2,
        compiler_params=params(),
        name="second_sum_b",
    )(got, kept, wg)


def line_sum_kernel(three_ref, two_ref, one_ref, zero_ref, feat_ref, wg_ref):
    width, part = feat_ref.shape[0], wg_ref.shape[0]
    for out, rows in ((wg_ref, pl.ds(width, part)), (feat_ref, pl.ds(0, width))):
        near = zero_ref[rows, :].astype(jnp.float32) + one_ref[rows, :].astype(jnp.float32)
        out[...] = near + (two_ref[rows, :].astype(jnp.float32) + three_ref[rows, :].astype(jnp.float32))


def line_sum(three, two, one, zero, width):
    total, piece = three.shape
    return pl.pallas_call(
        line_sum_kernel,
        in_specs=in_vmem(4),
        out_specs=in_vmem(2),
        out_shape=[
            jax.ShapeDtypeStruct((width, piece), jnp.float32),
            jax.ShapeDtypeStruct((total - width, piece), jnp.float32),
        ],
        compiler_params=params(),
        name="line_sum",
    )(three, two, one, zero)


def finish_kernel(feat_sum_ref, half_ref, other_ref, feat_ref, wg_ref):
    part = half_ref.shape[0]
    core = lax.rem(lax.axis_index("blk"), 2)
    wg_ref[pl.ds(pl.multiple_of(core * part, part), part), :] = half_ref[...]
    wg_ref[pl.ds(pl.multiple_of((1 - core) * part, part), part), :] = other_ref[...]
    feat_ref[...] = feat_sum_ref[...].T.astype(jnp.bfloat16)


def finish(feat_sum, half, other):
    return pl.pallas_call(
        finish_kernel,
        in_specs=in_vmem(3),
        out_specs=in_vmem(2),
        out_shape=[
            jax.ShapeDtypeStruct(feat_sum.shape[::-1], jnp.bfloat16),
            jax.ShapeDtypeStruct((2 * half.shape[0], half.shape[1]), jnp.float32),
        ],
        compiler_params=params(),
        name="finish",
    )(feat_sum, half, other)


class Layout:
    def __init__(self, n_blk, reps):
        self.n_blk, self.reps = n_blk, reps

    def route(self, moved):
        pairs = []
        for b in range(self.n_blk):
            for r in range(self.reps):
                to_b, to_r = moved(b, r)
                pairs.append((b * self.reps + r, to_b * self.reps + to_r))
        return pairs

    def owner_to_class(self, mask):
        reps = self.reps
        return self.route(lambda b, r: (((b // reps) ^ mask) * reps + (b + r) % reps, r))

    def class_to_owner(self, mask):
        reps = self.reps
        return self.route(lambda b, r: (((b // reps) ^ mask) * reps + (b - r) % reps, r))

    def in_class(self, mask):
        return self.route(lambda b, r: (b ^ (mask * self.reps), r))

    def along(self, first):
        reps = self.reps

        def moved(b, r):
            lane = (b - r) % reps
            mask, rep_mask = (0, 1) if (lane == 0) == first else (1, 0)
            to_r = r ^ rep_mask
            return (((b // reps) ^ mask) * reps + (lane + to_r) % reps, to_r)

        return self.route(moved)

    def plain(self, mask, rep_mask):
        return self.route(lambda b, r: (b ^ mask, r ^ rep_mask))


def send(value, route):
    return lax.ppermute(value, AXES, route)


def section_table(pos, count, blocks, flip):
    reps, n_blk = lax.axis_size("rep"), lax.axis_size("blk")
    b, r = lax.axis_index("blk"), lax.axis_index("rep")
    sections, slots = pos.shape
    columns = (b - r - jnp.arange(sections, dtype=jnp.int32) * reps) % n_blk
    places = (columns // reps) ^ (b // reps)
    live = jnp.arange(slots, dtype=jnp.int32)[None, :] < count[:, None]
    cells = jnp.where(live, pos ^ (flip * (blocks + 1)), -1)
    return jnp.concatenate([cells, places[:, None]], 1).astype(jnp.int32)


def local_pairs(features, weight, tiles, pos, count, cotangent):
    near, halves = 2, 2
    lay = Layout(lax.axis_size("blk"), lax.axis_size("rep"))
    b, r = lax.axis_index("blk"), lax.axis_index("rep")
    sections, tile = tiles.shape[0], tiles.shape[-1]
    rows, width = features.shape
    blocks, share = rows // tile, rows // halves
    table = section_table(pos, count, blocks, r * (blocks // halves))
    own_rows = lax.dynamic_slice_in_dim(features, r * share, share, 0)
    three, two, one, zero = [send(own_rows, lay.owner_to_class(at * near)) for at in (3, 2, 1, 0)]
    half_span = 2 * share
    far_cot = send(cotangent, lay.plain(0, 1))
    mine_a, mine_b = jnp.concatenate([zero, one], 0), jnp.concatenate([two, three], 0)
    mine_a, table = lax.optimization_barrier((mine_a, table))
    beside_a = send(mine_a, lay.along(False))
    beside_a, far_cot = lax.optimization_barrier((beside_a, far_cot))
    beside_b = send(mine_b, lay.along(False))
    across_a = send(jnp.concatenate([mine_a, beside_a], 0), lay.along(True))
    across_b = send(jnp.concatenate([mine_b, beside_b], 0), lay.along(True))

    dense, _ = dense_blocks(tiles, table, near, halves, blocks)

    def spans(at, units):
        return [(unit, at * half_span, row, half_span) for unit, row in units]

    local_units, far_units = [(0, 0), (1, 0)], [(2, 0), (3, half_span)]
    partial = aggregate(
        dense, spans(0, local_units + far_units) + spans(1, local_units),
        [mine_a, beside_a, across_a, across_a, mine_b, beside_b], None, jnp.float32)
    partial = aggregate(dense, spans(1, far_units), [across_b, across_b], partial, jnp.bfloat16)
    other = send(partial, lay.plain(0, 1))
    act, back, sent_a = turn(partial, other, weight, cotangent, far_cot, dense)

    got_a = send(sent_a, lay.along(True))
    sent_b, kept = rest_terms(back, dense)
    got_b = send(sent_b, lay.along(True))
    passed_a, kept_a = first_sum(half_span, got_a, kept, sent_a)
    passed_b, kept_b = first_sum(0, got_b, kept, sent_b)
    back_a = send(passed_a, lay.along(False))
    back_b = send(passed_b, lay.along(False))
    two, three, wg = second_sum_a(back_a, kept_a, passed_a)
    three = send(three, lay.class_to_owner(3 * near))
    two = send(two, lay.class_to_owner(2 * near))
    zero, one = second_sum_b(back_b, kept_b, wg)
    one = send(one, lay.class_to_owner(near))
    zero = send(zero, lay.class_to_owner(0))
    feat_sum, wg_half = line_sum(three, two, one, zero, width)
    wg_other = send(wg_half, lay.plain(1, 0))
    feat_grad, weight_grad = finish(feat_sum, wg_half, wg_other)
    return act, feat_grad, weight_grad


def local_any(features, weight, tiles, pos, count, cotangent):
    reps = lax.axis_size("rep")
    lay = Layout(lax.axis_size("blk"), reps)
    r = lax.axis_index("rep")
    sections, tile = tiles.shape[0], tiles.shape[-1]
    rows = features.shape[0]
    blocks, share = rows // tile, rows // reps
    bf = jnp.bfloat16

    line = jnp.concatenate([send(features, lay.owner_to_class(at)) for at in range(sections)], 0)
    dense, _ = dense_blocks(tiles, section_table(pos, count, blocks, 0), 1, 1, blocks)
    size = line.shape[0]
    partial = aggregate(dense, [(0, 0, 0, size)], [line], None, jnp.float32)
    g = lax.psum(partial, "rep").astype(bf)
    value, slope = gelu_and_slope(dot(g, weight))
    cot = lax.all_gather(cotangent, "rep", axis=0, tiled=True)
    grad = (cot.astype(jnp.float32) * slope).astype(bf)
    act = lax.dynamic_slice_in_dim(value, r * share, share, 0).astype(bf)
    own_g = lax.dynamic_slice_in_dim(g, r * share, share, 0)
    own_grad = lax.dynamic_slice_in_dim(grad, r * share, share, 0)
    weight_grad = lax.psum(tn_dot(own_g, own_grad), AXES)
    back = nt_dot(weight, grad).astype(bf)
    terms = dot(back, dense[0]).astype(bf)
    total = jnp.zeros((back.shape[0], rows), jnp.float32)
    for at in range(sections):
        total += send(terms[:, at * rows:(at + 1) * rows], lay.class_to_owner(at)).astype(jnp.float32)
    feat_grad = lax.psum_scatter(total.T, "rep", scatter_dimension=0, tiled=True).astype(bf)
    return act, feat_grad, weight_grad


def local(features, weight, tile_vals, tile_pos, tile_count, cotangent):
    tiles, pos, count = tile_vals[0, 0], tile_pos[0, 0], tile_count[0, 0]
    reps, tile = lax.axis_size("rep"), tiles.shape[-1]
    paired = reps == 2 and tiles.shape[0] == 8 and features.shape[0] % (2 * tile) == 0
    work = local_pairs if paired else local_any
    return work(features, weight, tiles, pos, count, cotangent)


def solution(mesh):
    placed = (
        P("blk", None),
        P(),
        P("blk", "rep", None, None, None, None),
        P("blk", "rep", None, None),
        P("blk", "rep", None),
        P(("blk", "rep"), None),
    )
    return jax.shard_map(
        local,
        mesh=mesh,
        in_specs=placed,
        out_specs=(P(("blk", "rep"), None), P(("blk", "rep"), None), P()),
        check_vma=False,
    )
```

```python
import functools

import jax
import jax.numpy as jnp
from jax import lax
from jax.experimental import pallas as pl
from jax.experimental.pallas import tpu as pltpu
from jax.sharding import PartitionSpec as P

AXES = ("blk", "rep")
VMEM_LIMIT = 16 * 1024 * 1024


def params():
    return pltpu.CompilerParams(vmem_limit_bytes=VMEM_LIMIT)


def in_vmem(count):
    return [pl.BlockSpec(memory_space=pltpu.VMEM)] * count


def held_in_vmem(value):
    return pltpu.with_memory_space_constraint(value, pltpu.VMEM)


def gelu_and_slope(v):
    scale = 0.7978845608028654
    square = v * v
    t = jnp.tanh(scale * (v + 0.044715 * (square * v)))
    half = 0.5 * (1.0 + t)
    slope = half + (0.5 * scale) * v * (1.0 - t * t) * (1.0 + 3.0 * 0.044715 * square)
    return v * half, slope


def nt_dot(a, b):
    return lax.dot_general(a, b, (((1,), (1,)), ((), ())), preferred_element_type=jnp.float32)


def tn_dot(a, b):
    return lax.dot_general(a, b, (((0,), (0,)), ((), ())), preferred_element_type=jnp.float32)


def dot(a, b):
    return jnp.dot(a, b, preferred_element_type=jnp.float32)


def split_by(value, size):
    if size & (size - 1):
        return lax.div(value, size), lax.rem(value, size)
    return lax.shift_right_logical(value, size.bit_length() - 1), value & (size - 1)


def dense_kernel(blocks, near, halves, table, tiles_ref, out_ref, held, arrived):
    sections, slots, tile = held.shape[0], held.shape[1], held.shape[-1]
    piece = out_ref.shape[2] // (sections // near)
    copies = [
        pltpu.make_async_copy(tiles_ref.at[section], held.at[section], arrived.at[section])
        for section in range(sections)
    ]
    for copy in copies:
        copy.start()
    out_ref[...] = jnp.zeros_like(out_ref)
    for section, copy in enumerate(copies):
        copy.wait()
        far_place, near_place = split_by(table[section, slots], near)
        for slot in range(slots):
            cell = table[section, slot]

            @pl.when(cell >= 0)
            def _():
                row, column = split_by(cell, blocks)
                half, column = split_by(column, blocks // halves)
                row_at = pl.multiple_of(row * tile, tile)
                column_at = pl.multiple_of(far_place * piece + column * tile, tile)
                out_ref[near_place * halves + half, pl.ds(row_at, tile), pl.ds(column_at, tile)] = held[section, slot]


def dense_blocks(tiles, table, near, halves, blocks):
    sections, _, tile, _ = tiles.shape
    rows = blocks * tile
    shape = (near * halves, rows, sections // near * rows // halves)
    return pl.pallas_call(
        functools.partial(dense_kernel, blocks, near, halves),
        in_specs=[pl.BlockSpec(memory_space=pltpu.SMEM), pl.BlockSpec(memory_space=pltpu.HBM)],
        out_specs=in_vmem(1)[0],
        out_shape=pltpu.VMEM(shape, jnp.bfloat16),
        scratch_shapes=[pltpu.VMEM(tiles.shape, tiles.dtype), pltpu.SemaphoreType.DMA((sections,))],
        compiler_params=params(),
        name="dense_blocks",
    )(table, pltpu.with_memory_space_constraint(tiles, pltpu.HBM))


def lane_of_class():
    return lax.rem(lax.axis_index("blk") + lax.axis_index("rep"), 2)


def unit_at(unit):
    if unit in (0, 3):
        return unit
    return 2 - lane_of_class() if unit == 1 else 1 + lane_of_class()


def aggregate_kernel(spans, based, dense_ref, *refs):
    given, out_ref = refs[:-1], refs[-1]
    total = given[0][...] if based else None
    halves = 2 if lax.axis_size("rep") == 2 and dense_ref.shape[0] > 1 else 1
    for at, first, start, base, size in spans:
        for half in range(halves):
            row = base if halves == 1 else pl.multiple_of(base + (half ^ lax.axis_index("rep")) * size, size)
            term = dot(dense_ref[first + half, :, pl.ds(start, size)], given[based + at][pl.ds(row, size), :])
            total = term if total is None else total + term
    out_ref[...] = total.astype(out_ref.dtype)


def aggregate(dense, spans, parts, base, dtype):
    rows, width = dense.shape[1], parts[0].shape[1]
    given = ([] if base is None else [base]) + parts
    return pl.pallas_call(
        functools.partial(aggregate_kernel, spans, len(given) - len(parts)),
        in_specs=in_vmem(1 + len(given)),
        out_specs=in_vmem(1)[0],
        out_shape=jax.ShapeDtypeStruct((rows, width), dtype),
        compiler_params=params(),
        name="aggregate",
    )(held_in_vmem(dense), *given)


def turn_kernel(share, chunk, own_ref, other_ref, weight_ref, cot_ref, far_cot_ref, dense_ref,
                act_ref, back_ref, sent_ref, g_ref, grad_ref):
    rows = own_ref.shape[0]
    weight = weight_ref[...]
    for half, cot in enumerate((cot_ref, far_cot_ref)):
        at, there = half * share, rows - share - half * share
        g = own_ref[pl.ds(at, share), :].astype(jnp.float32) + other_ref[pl.ds(there, share), :].astype(jnp.float32)
        g = g.astype(jnp.bfloat16)
        value, slope = gelu_and_slope(dot(g, weight))
        grad = (cot[...].astype(jnp.float32) * slope).astype(jnp.bfloat16)
        if half == 0:
            act_ref[...] = value.astype(jnp.bfloat16)
        g_ref[pl.ds(at, share), :] = g
        grad_ref[pl.ds(at, share), :] = grad
        back_ref[:, pl.ds(at, share)] = nt_dot(weight, grad).astype(jnp.bfloat16)
    back = back_ref[...]
    start, size = chunk
    for second in range(2):
        term = dot(back, dense_ref[unit_at(2 + second), :, pl.ds(start, size)])
        sent_ref[:, pl.ds(second * size, size)] = term.astype(jnp.bfloat16)
    part = sent_ref.shape[1] - 2 * size
    columns = pl.ds(pl.multiple_of(lane_of_class() * part, part), part)
    sent_ref[:, pl.ds(2 * size, part)] = tn_dot(g_ref[...], grad_ref[:, columns]).astype(jnp.bfloat16)


def turn(chunk, own, other, weight, cot, far_cot, dense):
    rows, width = own.shape
    share, hid = cot.shape
    bf = jnp.bfloat16
    return pl.pallas_call(
        functools.partial(turn_kernel, share, chunk),
        in_specs=in_vmem(6),
        out_specs=in_vmem(3),
        out_shape=[
            jax.ShapeDtypeStruct((share, hid), bf),
            jax.ShapeDtypeStruct((width, rows), bf),
            jax.ShapeDtypeStruct((width, 2 * chunk[1] + hid // 2), bf),
        ],
        scratch_shapes=[pltpu.VMEM((rows, width), bf), pltpu.VMEM((rows, hid), bf)],
        compiler_params=params(),
        name="turn",
    )(own, other, weight, cot, far_cot, held_in_vmem(dense))


def rest_kernel(chunks, back_ref, dense_ref, *refs):
    back = back_ref[...]
    for (start, size), sent in zip(chunks, refs[:-1]):
        for second in range(2):
            term = dot(back, dense_ref[unit_at(2 + second), :, pl.ds(start, size)])
            sent[:, pl.ds(second * size, size)] = term.astype(jnp.bfloat16)
    for second in range(2):
        refs[-1][second] = dot(back, dense_ref[unit_at(second)])


def rest_terms(chunks, back, dense):
    width, span = back.shape[0], dense.shape[2]
    return pl.pallas_call(
        functools.partial(rest_kernel, chunks),
        in_specs=in_vmem(2),
        out_specs=in_vmem(len(chunks) + 1),
        out_shape=[jax.ShapeDtypeStruct((width, 2 * size), jnp.bfloat16) for _, size in chunks]
        + [jax.ShapeDtypeStruct((2, width, span), jnp.float32)],
        compiler_params=params(),
        name="rest_terms",
    )(back, held_in_vmem(dense))


def first_sum_kernel(start, size, got_ref, kept_ref, own_ref, sent_ref, total_ref):
    extra = sent_ref.shape[1] - size
    total_ref[...] = kept_ref[0, :, pl.ds(start, size)] + got_ref[:, pl.ds(0, size)].astype(jnp.float32)
    passed = kept_ref[1, :, pl.ds(start, size)] + got_ref[:, pl.ds(size, size)].astype(jnp.float32)
    sent_ref[:, pl.ds(0, size)] = passed.astype(jnp.bfloat16)
    if extra:
        ours = own_ref[:, pl.ds(2 * size, extra)].astype(jnp.float32)
        theirs = got_ref[:, pl.ds(2 * size, extra)].astype(jnp.float32)
        sent_ref[:, pl.ds(size, extra)] = (ours + theirs).astype(jnp.bfloat16)


def first_sum(chunk, got, kept, own):
    width = kept.shape[1]
    start, size = chunk
    extra = got.shape[1] - 2 * size
    return pl.pallas_call(
        functools.partial(first_sum_kernel, start, size),
        in_specs=in_vmem(3),
        out_specs=in_vmem(2),
        out_shape=[
            jax.ShapeDtypeStruct((width, size + extra), jnp.bfloat16),
            jax.ShapeDtypeStruct((width, size), jnp.float32),
        ],
        compiler_params=params(),
        name="first_sum",
    )(got, kept, own)


def second_sum_kernel(got_ref, kept_ref, own_ref, two_ref, three_ref, wg_ref):
    piece = kept_ref.shape[1] // 2
    part = two_ref.shape[1] - piece
    tail = pl.ds(2 * piece, part)
    wg = own_ref[:, tail].astype(jnp.float32) + got_ref[:, tail].astype(jnp.float32)
    wg_ref[...] = wg.astype(jnp.bfloat16)
    for at, out in enumerate((two_ref, three_ref)):
        span = pl.ds(at * piece, piece)
        out[:, pl.ds(0, piece)] = (kept_ref[:, span] + got_ref[:, span].astype(jnp.float32)).astype(jnp.bfloat16)
        out[:, pl.ds(piece, part)] = wg.astype(jnp.bfloat16)


def second_sum(got, kept, own):
    width, size = kept.shape
    message = jax.ShapeDtypeStruct((width, got.shape[1] - size // 2), jnp.bfloat16)
    return pl.pallas_call(
        second_sum_kernel,
        in_specs=in_vmem(3),
        out_specs=in_vmem(3),
        out_shape=[message] * 2 + [jax.ShapeDtypeStruct((width, got.shape[1] - size), jnp.bfloat16)],
        compiler_params=params(),
        name="second_sum",
    )(got, kept, own)


def last_sum_kernel(got_ref, kept_ref, wg_ref, zero_ref, one_ref):
    piece = zero_ref.shape[1]
    tail = pl.ds(piece, one_ref.shape[1] - piece)
    zero_ref[...] = kept_ref[:, pl.ds(0, piece)] + got_ref[:, pl.ds(0, piece)].astype(jnp.float32)
    span = pl.ds(piece, piece)
    one_ref[:, pl.ds(0, piece)] = (kept_ref[:, span] + got_ref[:, span].astype(jnp.float32)).astype(jnp.bfloat16)
    one_ref[:, tail] = wg_ref[...]


def last_sum(got, kept, wg):
    width, size = kept.shape
    return pl.pallas_call(
        last_sum_kernel,
        in_specs=in_vmem(3),
        out_specs=in_vmem(2),
        out_shape=[
            jax.ShapeDtypeStruct((width, size // 2), jnp.float32),
            jax.ShapeDtypeStruct((width, size // 2 + wg.shape[1]), jnp.bfloat16),
        ],
        compiler_params=params(),
        name="last_sum",
    )(got, kept, wg)


def line_sum_kernel(three_ref, two_ref, one_ref, sent_one_ref, zero_ref, out_ref):
    piece = zero_ref.shape[1]
    span, tail = pl.ds(0, piece), pl.ds(piece, out_ref.shape[1] - piece)
    three, two, one = [ref[:, span].astype(jnp.float32) for ref in (three_ref, two_ref, one_ref)]
    out_ref[:, span] = ((zero_ref[...] + one) + (two + three)).astype(jnp.bfloat16)
    three, two, one, own = [ref[:, tail].astype(jnp.float32) for ref in (three_ref, two_ref, one_ref, sent_one_ref)]
    out_ref[:, tail] = ((own + one) + (two + three)).astype(jnp.bfloat16)


def line_sum(three, two, one, sent_one, zero):
    return pl.pallas_call(
        line_sum_kernel,
        in_specs=in_vmem(5),
        out_specs=in_vmem(1)[0],
        out_shape=jax.ShapeDtypeStruct(two.shape, jnp.bfloat16),
        compiler_params=params(),
        name="line_sum",
    )(three, two, one, sent_one, zero)


def finish_kernel(own_ref, got_ref, feat_ref, wg_ref):
    piece = feat_ref.shape[0]
    part = own_ref.shape[1] - piece
    lane = lane_of_class()
    wg_ref[:, pl.ds(pl.multiple_of(lane * part, part), part)] = own_ref[:, pl.ds(piece, part)].astype(jnp.float32)
    wg_ref[:, pl.ds(pl.multiple_of((1 - lane) * part, part), part)] = got_ref[:, pl.ds(piece, part)].astype(jnp.float32)
    span = pl.ds(0, piece)
    ours = jnp.where(lax.axis_index("rep") == 0, own_ref[:, span].astype(jnp.float32), got_ref[:, span].astype(jnp.float32))
    feat_ref[...] = ours.T.astype(jnp.bfloat16)


def finish(own, got, piece):
    width, total = own.shape
    return pl.pallas_call(
        finish_kernel,
        in_specs=in_vmem(2),
        out_specs=in_vmem(2),
        out_shape=[
            jax.ShapeDtypeStruct((piece, width), jnp.bfloat16),
            jax.ShapeDtypeStruct((width, 2 * (total - piece)), jnp.float32),
        ],
        compiler_params=params(),
        name="finish",
    )(own, got)


class Layout:
    def __init__(self, n_blk, reps):
        self.n_blk, self.reps = n_blk, reps

    def route(self, moved):
        pairs = []
        for b in range(self.n_blk):
            for r in range(self.reps):
                to_b, to_r = moved(b, r)
                pairs.append((b * self.reps + r, to_b * self.reps + to_r))
        return pairs

    def owner_to_class(self, mask):
        reps = self.reps
        return self.route(lambda b, r: (((b // reps) ^ mask) * reps + (b + r) % reps, r))

    def class_to_owner(self, mask):
        reps = self.reps
        return self.route(lambda b, r: (((b // reps) ^ mask) * reps + (b - r) % reps, r))

    def in_class(self, mask):
        return self.route(lambda b, r: (b ^ (mask * self.reps), r))

    def along(self, first):
        reps = self.reps

        def moved(b, r):
            lane = (b - r) % reps
            mask, rep_mask = (0, 1) if (lane == 0) == first else (1, 0)
            to_r = r ^ rep_mask
            return (((b // reps) ^ mask) * reps + (lane + to_r) % reps, to_r)

        return self.route(moved)

    def plain(self, mask, rep_mask):
        return self.route(lambda b, r: (b ^ mask, r ^ rep_mask))


def send(value, route):
    return lax.ppermute(value, AXES, route)


def section_table(pos, count, blocks, flip):
    reps, n_blk = lax.axis_size("rep"), lax.axis_size("blk")
    b, r = lax.axis_index("blk"), lax.axis_index("rep")
    sections, slots = pos.shape
    columns = (b - r - jnp.arange(sections, dtype=jnp.int32) * reps) % n_blk
    places = (columns // reps) ^ (b // reps)
    live = jnp.arange(slots, dtype=jnp.int32)[None, :] < count[:, None]
    cells = jnp.where(live, pos ^ (flip * (blocks + 1)), -1)
    return jnp.concatenate([cells, places[:, None]], 1).astype(jnp.int32)


def local_pairs(features, weight, tiles, pos, count, cotangent):
    near, halves = 2, 2
    lay = Layout(lax.axis_size("blk"), lax.axis_size("rep"))
    b, r = lax.axis_index("blk"), lax.axis_index("rep")
    sections, tile = tiles.shape[0], tiles.shape[-1]
    rows, width = features.shape
    blocks, share = rows // tile, rows // halves
    table = section_table(pos, count, blocks, r * (blocks // halves))
    two, one = [send(features, lay.owner_to_class(at * near)) for at in (2, 1)]
    whole, whole_beside = [send(features, lay.owner_to_class(at)) for at in range(2)]
    far_cot = send(cotangent, lay.plain(0, 1))
    three = send(two, lay.in_class(near))
    mine = jnp.concatenate([one, two], 0)
    beside = send(mine, lay.in_class(1))
    beside_three = send(three, lay.in_class(1))
    dense = dense_blocks(tiles, table, near, halves, blocks)
    spans = [(0, 0, 0, 0, share), (1, 2, 0, 0, share), (2, 0, share, 0, share), (2, 0, 2 * share, rows, share),
             (3, 2, share, 0, share), (3, 2, 2 * share, rows, share), (4, 0, 3 * share, 0, share)]
    partial = aggregate(dense, spans, [whole, whole_beside, mine, beside, three], None, jnp.float32)
    partial = aggregate(dense, [(0, 2, 3 * share, 0, share)], [beside_three], partial, jnp.bfloat16)
    other = send(partial, lay.plain(0, 1))
    chunk_a, chunk_b = (2 * share, 2 * share), (0, 2 * share)
    act, back, sent_a = turn(chunk_a, partial, other, weight, cotangent, far_cot, dense)
    got_a = send(sent_a, lay.along(True))
    sent_b, kept = rest_terms([chunk_b], back, dense)
    got_b = send(sent_b, lay.along(True))
    passed_a, kept_a = first_sum(chunk_a, got_a, kept, sent_a)
    back_a = send(passed_a, lay.along(False))
    passed_b, kept_b = first_sum(chunk_b, got_b, kept, sent_b)
    back_b = send(passed_b, lay.along(False))
    sent_two, sent_three, wg = second_sum(back_a, kept_a, passed_a)
    three = send(sent_three, lay.in_class(3 * near))
    two = send(sent_two, lay.in_class(2 * near))
    zero, sent_one = last_sum(back_b, kept_b, wg)
    one = send(sent_one, lay.in_class(near))
    ours = line_sum(three, two, one, sent_one, zero)
    feat_grad, weight_grad = finish(ours, send(ours, lay.plain(1, 0)), share)
    return act, feat_grad, weight_grad


def local_any(features, weight, tiles, pos, count, cotangent):
    reps = lax.axis_size("rep")
    lay = Layout(lax.axis_size("blk"), reps)
    r = lax.axis_index("rep")
    sections, tile = tiles.shape[0], tiles.shape[-1]
    rows = features.shape[0]
    blocks, share = rows // tile, rows // reps
    bf = jnp.bfloat16

    line = jnp.concatenate([send(features, lay.owner_to_class(at)) for at in range(sections)], 0)
    dense = dense_blocks(tiles, section_table(pos, count, blocks, 0), 1, 1, blocks)
    size = line.shape[0]
    partial = aggregate(dense, [(0, 0, 0, 0, size)], [line], None, jnp.float32)
    g = lax.psum(partial, "rep").astype(bf)
    value, slope = gelu_and_slope(dot(g, weight))
    cot = lax.all_gather(cotangent, "rep", axis=0, tiled=True)
    grad = (cot.astype(jnp.float32) * slope).astype(bf)
    act = lax.dynamic_slice_in_dim(value, r * share, share, 0).astype(bf)
    own_g = lax.dynamic_slice_in_dim(g, r * share, share, 0)
    own_grad = lax.dynamic_slice_in_dim(grad, r * share, share, 0)
    weight_grad = lax.psum(tn_dot(own_g, own_grad), AXES)
    back = nt_dot(weight, grad).astype(bf)
    terms = dot(back, dense[0]).astype(bf)
    total = jnp.zeros((back.shape[0], rows), jnp.float32)
    for at in range(sections):
        total += send(terms[:, at * rows:(at + 1) * rows], lay.class_to_owner(at)).astype(jnp.float32)
    feat_grad = lax.psum_scatter(total.T, "rep", scatter_dimension=0, tiled=True).astype(bf)
    return act, feat_grad, weight_grad


def local(features, weight, tile_vals, tile_pos, tile_count, cotangent):
    tiles, pos, count = tile_vals[0, 0], tile_pos[0, 0], tile_count[0, 0]
    reps, tile = lax.axis_size("rep"), tiles.shape[-1]
    paired = reps == 2 and tiles.shape[0] == 8 and features.shape[0] % (2 * tile) == 0
    work = local_pairs if paired else local_any
    return work(features, weight, tiles, pos, count, cotangent)


def solution(mesh):
    placed = (
        P("blk", None),
        P(),
        P("blk", "rep", None, None, None, None),
        P("blk", "rep", None, None),
        P("blk", "rep", None),
        P(("blk", "rep"), None),
    )
    return jax.shard_map(
        local,
        mesh=mesh,
        in_specs=placed,
        out_specs=(P(("blk", "rep"), None), P(("blk", "rep"), None), P()),
        check_vma=False,
    )
```

```python
import functools

import jax
import jax.numpy as jnp
from jax import lax
from jax.experimental import pallas as pl
from jax.experimental.pallas import tpu as pltpu
from jax.sharding import PartitionSpec as P

AXES = ("blk", "rep")
VMEM_LIMIT = 16 * 1024 * 1024


def params():
    return pltpu.CompilerParams(vmem_limit_bytes=VMEM_LIMIT)


def in_vmem(count):
    return [pl.BlockSpec(memory_space=pltpu.VMEM)] * count


def held_in_vmem(value):
    return pltpu.with_memory_space_constraint(value, pltpu.VMEM)


def gelu_and_slope(v):
    scale = 0.7978845608028654
    square = v * v
    t = jnp.tanh(scale * (v + 0.044715 * (square * v)))
    half = 0.5 * (1.0 + t)
    slope = half + (0.5 * scale) * v * (1.0 - t * t) * (1.0 + 3.0 * 0.044715 * square)
    return v * half, slope


def nt_dot(a, b):
    return lax.dot_general(a, b, (((1,), (1,)), ((), ())), preferred_element_type=jnp.float32)


def tn_dot(a, b):
    return lax.dot_general(a, b, (((0,), (0,)), ((), ())), preferred_element_type=jnp.float32)


def dot(a, b):
    return jnp.dot(a, b, preferred_element_type=jnp.float32)


def split_by(value, size):
    if size & (size - 1):
        return lax.div(value, size), lax.rem(value, size)
    return lax.shift_right_logical(value, size.bit_length() - 1), value & (size - 1)


def dense_kernel(blocks, near, halves, table, tiles_ref, out_ref, held, arrived):
    sections, slots, tile = held.shape[0], held.shape[1], held.shape[-1]
    piece = out_ref.shape[2] // (sections // near)
    copies = [
        pltpu.make_async_copy(tiles_ref.at[section], held.at[section], arrived.at[section])
        for section in range(sections)
    ]
    for copy in copies:
        copy.start()
    out_ref[...] = jnp.zeros_like(out_ref)
    for section, copy in enumerate(copies):
        copy.wait()
        far_place, near_place = split_by(table[section, slots], near)
        for slot in range(slots):
            cell = table[section, slot]

            @pl.when(cell >= 0)
            def _():
                row, column = split_by(cell, blocks)
                half, column = split_by(column, blocks // halves)
                row_at = pl.multiple_of(row * tile, tile)
                column_at = pl.multiple_of(far_place * piece + column * tile, tile)
                out_ref[near_place * halves + half, pl.ds(row_at, tile), pl.ds(column_at, tile)] = held[section, slot]


def dense_blocks(tiles, table, near, halves, blocks):
    sections, _, tile, _ = tiles.shape
    rows = blocks * tile
    shape = (near * halves, rows, sections // near * rows // halves)
    return pl.pallas_call(
        functools.partial(dense_kernel, blocks, near, halves),
        in_specs=[pl.BlockSpec(memory_space=pltpu.SMEM), pl.BlockSpec(memory_space=pltpu.HBM)],
        out_specs=in_vmem(1)[0],
        out_shape=pltpu.VMEM(shape, jnp.bfloat16),
        scratch_shapes=[pltpu.VMEM(tiles.shape, tiles.dtype), pltpu.SemaphoreType.DMA((sections,))],
        compiler_params=params(),
        name="dense_blocks",
    )(table, pltpu.with_memory_space_constraint(tiles, pltpu.HBM))


def lane_of_class():
    return lax.rem(lax.axis_index("blk") + lax.axis_index("rep"), 2)


def unit_at(unit):
    if unit in (0, 3):
        return unit
    return 2 - lane_of_class() if unit == 1 else 1 + lane_of_class()


def aggregate_kernel(spans, based, dense_ref, *refs):
    given, out_ref = refs[:-1], refs[-1]
    total = given[0][...] if based else None
    halves = 2 if lax.axis_size("rep") == 2 and dense_ref.shape[0] > 1 else 1
    for at, first, start, base, size in spans:
        for half in range(halves):
            row = base if halves == 1 else pl.multiple_of(base + (half ^ lax.axis_index("rep")) * size, size)
            term = dot(dense_ref[first + half, :, pl.ds(start, size)], given[based + at][pl.ds(row, size), :])
            total = term if total is None else total + term
    out_ref[...] = total.astype(out_ref.dtype)


def aggregate(dense, spans, parts, base, dtype):
    rows, width = dense.shape[1], parts[0].shape[1]
    given = ([] if base is None else [base]) + parts
    return pl.pallas_call(
        functools.partial(aggregate_kernel, spans, len(given) - len(parts)),
        in_specs=in_vmem(1 + len(given)),
        out_specs=in_vmem(1)[0],
        out_shape=jax.ShapeDtypeStruct((rows, width), dtype),
        compiler_params=params(),
        name="aggregate",
    )(held_in_vmem(dense), *given)


def turn_kernel(share, chunk, own_ref, other_ref, weight_ref, cot_ref, far_cot_ref, dense_ref,
                act_ref, back_ref, sent_ref, g_ref, grad_ref):
    rows = own_ref.shape[0]
    weight = weight_ref[...]
    for half, cot in enumerate((cot_ref, far_cot_ref)):
        at, there = half * share, rows - share - half * share
        g = own_ref[pl.ds(at, share), :].astype(jnp.float32) + other_ref[pl.ds(there, share), :].astype(jnp.float32)
        g = g.astype(jnp.bfloat16)
        value, slope = gelu_and_slope(dot(g, weight))
        grad = (cot[...].astype(jnp.float32) * slope).astype(jnp.bfloat16)
        if half == 0:
            act_ref[...] = value.astype(jnp.bfloat16)
        g_ref[pl.ds(at, share), :] = g
        grad_ref[pl.ds(at, share), :] = grad
        back_ref[:, pl.ds(at, share)] = nt_dot(weight, grad).astype(jnp.bfloat16)
    back = back_ref[...]
    start, size = chunk
    for second in range(2):
        term = dot(back, dense_ref[unit_at(2 + second), :, pl.ds(start, size)])
        sent_ref[:, pl.ds(second * size, size)] = term.astype(jnp.bfloat16)
    part = sent_ref.shape[1] - 2 * size
    columns = pl.ds(pl.multiple_of(lane_of_class() * part, part), part)
    sent_ref[:, pl.ds(2 * size, part)] = tn_dot(g_ref[...], grad_ref[:, columns]).astype(jnp.bfloat16)


def turn(chunk, own, other, weight, cot, far_cot, dense):
    rows, width = own.shape
    share, hid = cot.shape
    bf = jnp.bfloat16
    return pl.pallas_call(
        functools.partial(turn_kernel, share, chunk),
        in_specs=in_vmem(6),
        out_specs=in_vmem(3),
        out_shape=[
            jax.ShapeDtypeStruct((share, hid), bf),
            jax.ShapeDtypeStruct((width, rows), bf),
            jax.ShapeDtypeStruct((width, 2 * chunk[1] + hid // 2), bf),
        ],
        scratch_shapes=[pltpu.VMEM((rows, width), bf), pltpu.VMEM((rows, hid), bf)],
        compiler_params=params(),
        name="turn",
    )(own, other, weight, cot, far_cot, held_in_vmem(dense))


def rest_kernel(chunks, back_ref, dense_ref, *refs):
    back = back_ref[...]
    for (start, size), sent in zip(chunks, refs[:-1]):
        for second in range(2):
            term = dot(back, dense_ref[unit_at(2 + second), :, pl.ds(start, size)])
            sent[:, pl.ds(second * size, size)] = term.astype(jnp.bfloat16)
    for second in range(2):
        refs[-1][second] = dot(back, dense_ref[unit_at(second)])


def rest_terms(chunks, back, dense):
    width, span = back.shape[0], dense.shape[2]
    return pl.pallas_call(
        functools.partial(rest_kernel, chunks),
        in_specs=in_vmem(2),
        out_specs=in_vmem(len(chunks) + 1),
        out_shape=[jax.ShapeDtypeStruct((width, 2 * size), jnp.bfloat16) for _, size in chunks]
        + [jax.ShapeDtypeStruct((2, width, span), jnp.float32)],
        compiler_params=params(),
        name="rest_terms",
    )(back, held_in_vmem(dense))


def first_sum_kernel(start, size, got_ref, kept_ref, own_ref, sent_ref, total_ref):
    extra = sent_ref.shape[1] - size
    total_ref[...] = kept_ref[0, :, pl.ds(start, size)] + got_ref[:, pl.ds(0, size)].astype(jnp.float32)
    passed = kept_ref[1, :, pl.ds(start, size)] + got_ref[:, pl.ds(size, size)].astype(jnp.float32)
    sent_ref[:, pl.ds(0, size)] = passed.astype(jnp.bfloat16)
    if extra:
        ours = own_ref[:, pl.ds(2 * size, extra)].astype(jnp.float32)
        theirs = got_ref[:, pl.ds(2 * size, extra)].astype(jnp.float32)
        sent_ref[:, pl.ds(size, extra)] = (ours + theirs).astype(jnp.bfloat16)


def first_sum(chunk, got, kept, own):
    width = kept.shape[1]
    start, size = chunk
    extra = got.shape[1] - 2 * size
    return pl.pallas_call(
        functools.partial(first_sum_kernel, start, size),
        in_specs=in_vmem(3),
        out_specs=in_vmem(2),
        out_shape=[
            jax.ShapeDtypeStruct((width, size + extra), jnp.bfloat16),
            jax.ShapeDtypeStruct((width, size), jnp.float32),
        ],
        compiler_params=params(),
        name="first_sum",
    )(got, kept, own)


def second_sum_kernel(got_ref, kept_ref, own_ref, two_ref, three_ref, wg_ref):
    piece = kept_ref.shape[1] // 2
    part = two_ref.shape[1] - piece
    tail = pl.ds(2 * piece, part)
    wg = own_ref[:, tail].astype(jnp.float32) + got_ref[:, tail].astype(jnp.float32)
    wg_ref[...] = wg.astype(jnp.bfloat16)
    for at, out in enumerate((two_ref, three_ref)):
        span = pl.ds(at * piece, piece)
        out[:, pl.ds(0, piece)] = (kept_ref[:, span] + got_ref[:, span].astype(jnp.float32)).astype(jnp.bfloat16)
        out[:, pl.ds(piece, part)] = wg.astype(jnp.bfloat16)


def second_sum(got, kept, own):
    width, size = kept.shape
    message = jax.ShapeDtypeStruct((width, got.shape[1] - size // 2), jnp.bfloat16)
    return pl.pallas_call(
        second_sum_kernel,
        in_specs=in_vmem(3),
        out_specs=in_vmem(3),
        out_shape=[message] * 2 + [jax.ShapeDtypeStruct((width, got.shape[1] - size), jnp.bfloat16)],
        compiler_params=params(),
        name="second_sum",
    )(got, kept, own)


def last_sum_kernel(got_ref, kept_ref, wg_ref, zero_ref, one_ref):
    piece = zero_ref.shape[1]
    tail = pl.ds(piece, one_ref.shape[1] - piece)
    zero_ref[...] = kept_ref[:, pl.ds(0, piece)] + got_ref[:, pl.ds(0, piece)].astype(jnp.float32)
    span = pl.ds(piece, piece)
    one_ref[:, pl.ds(0, piece)] = (kept_ref[:, span] + got_ref[:, span].astype(jnp.float32)).astype(jnp.bfloat16)
    one_ref[:, tail] = wg_ref[...]


def last_sum(got, kept, wg):
    width, size = kept.shape
    return pl.pallas_call(
        last_sum_kernel,
        in_specs=in_vmem(3),
        out_specs=in_vmem(2),
        out_shape=[
            jax.ShapeDtypeStruct((width, size // 2), jnp.float32),
            jax.ShapeDtypeStruct((width, size // 2 + wg.shape[1]), jnp.bfloat16),
        ],
        compiler_params=params(),
        name="last_sum",
    )(got, kept, wg)


def line_sum_kernel(three_ref, two_ref, one_ref, sent_one_ref, zero_ref, out_ref):
    piece = zero_ref.shape[1]
    span, tail = pl.ds(0, piece), pl.ds(piece, out_ref.shape[1] - piece)
    three, two, one = [ref[:, span].astype(jnp.float32) for ref in (three_ref, two_ref, one_ref)]
    out_ref[:, span] = ((zero_ref[...] + one) + (two + three)).astype(jnp.bfloat16)
    three, two, one, own = [ref[:, tail].astype(jnp.float32) for ref in (three_ref, two_ref, one_ref, sent_one_ref)]
    out_ref[:, tail] = ((own + one) + (two + three)).astype(jnp.bfloat16)


def line_sum(three, two, one, sent_one, zero):
    return pl.pallas_call(
        line_sum_kernel,
        in_specs=in_vmem(5),
        out_specs=in_vmem(1)[0],
        out_shape=jax.ShapeDtypeStruct(two.shape, jnp.bfloat16),
        compiler_params=params(),
        name="line_sum",
    )(three, two, one, sent_one, zero)


def finish_kernel(own_ref, got_ref, feat_ref, wg_ref):
    piece = feat_ref.shape[0]
    part = own_ref.shape[1] - piece
    lane = lane_of_class()
    wg_ref[:, pl.ds(pl.multiple_of(lane * part, part), part)] = own_ref[:, pl.ds(piece, part)].astype(jnp.float32)
    wg_ref[:, pl.ds(pl.multiple_of((1 - lane) * part, part), part)] = got_ref[:, pl.ds(piece, part)].astype(jnp.float32)
    span = pl.ds(0, piece)
    ours = jnp.where(lax.axis_index("rep") == 0, own_ref[:, span].astype(jnp.float32), got_ref[:, span].astype(jnp.float32))
    feat_ref[...] = ours.T.astype(jnp.bfloat16)


def finish(own, got, piece):
    width, total = own.shape
    return pl.pallas_call(
        finish_kernel,
        in_specs=in_vmem(2),
        out_specs=in_vmem(2),
        out_shape=[
            jax.ShapeDtypeStruct((piece, width), jnp.bfloat16),
            jax.ShapeDtypeStruct((width, 2 * (total - piece)), jnp.float32),
        ],
        compiler_params=params(),
        name="finish",
    )(own, got)


class Layout:
    def __init__(self, n_blk, reps):
        self.n_blk, self.reps = n_blk, reps

    def route(self, moved):
        pairs = []
        for b in range(self.n_blk):
            for r in range(self.reps):
                to_b, to_r = moved(b, r)
                pairs.append((b * self.reps + r, to_b * self.reps + to_r))
        return pairs

    def owner_to_class(self, mask):
        reps = self.reps
        return self.route(lambda b, r: (((b // reps) ^ mask) * reps + (b + r) % reps, r))

    def class_to_owner(self, mask):
        reps = self.reps
        return self.route(lambda b, r: (((b // reps) ^ mask) * reps + (b - r) % reps, r))

    def in_class(self, mask):
        return self.route(lambda b, r: (b ^ (mask * self.reps), r))

    def along(self, first):
        reps = self.reps

        def moved(b, r):
            lane = (b - r) % reps
            mask, rep_mask = (0, 1) if (lane == 0) == first else (1, 0)
            to_r = r ^ rep_mask
            return (((b // reps) ^ mask) * reps + (lane + to_r) % reps, to_r)

        return self.route(moved)

    def plain(self, mask, rep_mask):
        return self.route(lambda b, r: (b ^ mask, r ^ rep_mask))


def send(value, route):
    return lax.ppermute(value, AXES, route)


def section_table(pos, count, blocks, flip):
    reps, n_blk = lax.axis_size("rep"), lax.axis_size("blk")
    b, r = lax.axis_index("blk"), lax.axis_index("rep")
    sections, slots = pos.shape
    columns = (b - r - jnp.arange(sections, dtype=jnp.int32) * reps) % n_blk
    places = (columns // reps) ^ (b // reps)
    live = jnp.arange(slots, dtype=jnp.int32)[None, :] < count[:, None]
    cells = jnp.where(live, pos ^ (flip * (blocks + 1)), -1)
    return jnp.concatenate([cells, places[:, None]], 1).astype(jnp.int32)


def local_pairs(features, weight, tiles, pos, count, cotangent):
    near, halves = 2, 2
    lay = Layout(lax.axis_size("blk"), lax.axis_size("rep"))
    b, r = lax.axis_index("blk"), lax.axis_index("rep")
    sections, tile = tiles.shape[0], tiles.shape[-1]
    rows, width = features.shape
    blocks, share = rows // tile, rows // halves
    table = section_table(pos, count, blocks, r * (blocks // halves))
    two, one = [send(features, lay.owner_to_class(at * near)) for at in (2, 1)]
    whole, whole_beside = [send(features, lay.owner_to_class(at)) for at in range(2)]
    far_cot = send(cotangent, lay.plain(0, 1))
    three = send(two, lay.in_class(near))
    mine = jnp.concatenate([two, one], 0)
    beside = send(mine, lay.in_class(1))
    beside_three = send(three, lay.in_class(1))
    dense = dense_blocks(tiles, table, near, halves, blocks)
    spans = [(0, 0, 0, 0, share), (1, 2, 0, 0, share), (2, 0, 2 * share, 0, share), (2, 0, share, rows, share),
             (3, 2, 2 * share, 0, share), (3, 2, share, rows, share), (4, 0, 3 * share, 0, share)]
    partial = aggregate(dense, spans, [whole, whole_beside, mine, beside, three], None, jnp.float32)
    partial = aggregate(dense, [(0, 2, 3 * share, 0, share)], [beside_three], partial, jnp.bfloat16)
    other = send(partial, lay.plain(0, 1))
    chunk_a, chunk_b = (2 * share, 2 * share), (0, 2 * share)
    act, back, sent_a = turn(chunk_a, partial, other, weight, cotangent, far_cot, dense)
    got_a = send(sent_a, lay.along(True))
    sent_b, kept = rest_terms([chunk_b], back, dense)
    got_b = send(sent_b, lay.along(True))
    passed_a, kept_a = first_sum(chunk_a, got_a, kept, sent_a)
    back_a = send(passed_a, lay.along(False))
    passed_b, kept_b = first_sum(chunk_b, got_b, kept, sent_b)
    back_b = send(passed_b, lay.along(False))
    sent_two, sent_three, wg = second_sum(back_a, kept_a, passed_a)
    three = send(sent_three, lay.in_class(3 * near))
    two = send(sent_two, lay.in_class(2 * near))
    zero, sent_one = last_sum(back_b, kept_b, wg)
    one = send(sent_one, lay.in_class(near))
    ours = line_sum(three, two, one, sent_one, zero)
    feat_grad, weight_grad = finish(ours, send(ours, lay.plain(1, 0)), share)
    return act, feat_grad, weight_grad


def local_any(features, weight, tiles, pos, count, cotangent):
    reps = lax.axis_size("rep")
    lay = Layout(lax.axis_size("blk"), reps)
    r = lax.axis_index("rep")
    sections, tile = tiles.shape[0], tiles.shape[-1]
    rows = features.shape[0]
    blocks, share = rows // tile, rows // reps
    bf = jnp.bfloat16

    line = jnp.concatenate([send(features, lay.owner_to_class(at)) for at in range(sections)], 0)
    dense = dense_blocks(tiles, section_table(pos, count, blocks, 0), 1, 1, blocks)
    size = line.shape[0]
    partial = aggregate(dense, [(0, 0, 0, 0, size)], [line], None, jnp.float32)
    g = lax.psum(partial, "rep").astype(bf)
    value, slope = gelu_and_slope(dot(g, weight))
    cot = lax.all_gather(cotangent, "rep", axis=0, tiled=True)
    grad = (cot.astype(jnp.float32) * slope).astype(bf)
    act = lax.dynamic_slice_in_dim(value, r * share, share, 0).astype(bf)
    own_g = lax.dynamic_slice_in_dim(g, r * share, share, 0)
    own_grad = lax.dynamic_slice_in_dim(grad, r * share, share, 0)
    weight_grad = lax.psum(tn_dot(own_g, own_grad), AXES)
    back = nt_dot(weight, grad).astype(bf)
    terms = dot(back, dense[0]).astype(bf)
    total = jnp.zeros((back.shape[0], rows), jnp.float32)
    for at in range(sections):
        total += send(terms[:, at * rows:(at + 1) * rows], lay.class_to_owner(at)).astype(jnp.float32)
    feat_grad = lax.psum_scatter(total.T, "rep", scatter_dimension=0, tiled=True).astype(bf)
    return act, feat_grad, weight_grad


def local(features, weight, tile_vals, tile_pos, tile_count, cotangent):
    tiles, pos, count = tile_vals[0, 0], tile_pos[0, 0], tile_count[0, 0]
    reps, tile = lax.axis_size("rep"), tiles.shape[-1]
    paired = reps == 2 and tiles.shape[0] == 8 and features.shape[0] % (2 * tile) == 0
    work = local_pairs if paired else local_any
    return work(features, weight, tiles, pos, count, cotangent)


def solution(mesh):
    placed = (
        P("blk", None),
        P(),
        P("blk", "rep", None, None, None, None),
        P("blk", "rep", None, None),
        P("blk", "rep", None),
        P(("blk", "rep"), None),
    )
    return jax.shard_map(
        local,
        mesh=mesh,
        in_specs=placed,
        out_specs=(P(("blk", "rep"), None), P(("blk", "rep"), None), P()),
        check_vma=False,
    )
```

```python
import functools

import jax
import jax.numpy as jnp
from jax import lax
from jax.experimental import pallas as pl
from jax.experimental.pallas import tpu as pltpu
from jax.sharding import PartitionSpec as P

AXES = ("blk", "rep")
VMEM_LIMIT = 16 * 1024 * 1024


def params():
    return pltpu.CompilerParams(vmem_limit_bytes=VMEM_LIMIT)


def in_vmem(count):
    return [pl.BlockSpec(memory_space=pltpu.VMEM)] * count


def held_in_vmem(value):
    return pltpu.with_memory_space_constraint(value, pltpu.VMEM)


def gelu_and_slope(v):
    scale = 0.7978845608028654
    square = v * v
    t = jnp.tanh(scale * (v + 0.044715 * (square * v)))
    half = 0.5 * (1.0 + t)
    slope = half + (0.5 * scale) * v * (1.0 - t * t) * (1.0 + 3.0 * 0.044715 * square)
    return v * half, slope


def nt_dot(a, b):
    return lax.dot_general(a, b, (((1,), (1,)), ((), ())), preferred_element_type=jnp.float32)


def tn_dot(a, b):
    return lax.dot_general(a, b, (((0,), (0,)), ((), ())), preferred_element_type=jnp.float32)


def dot(a, b):
    return jnp.dot(a, b, preferred_element_type=jnp.float32)


def split_by(value, size):
    if size & (size - 1):
        return lax.div(value, size), lax.rem(value, size)
    return lax.shift_right_logical(value, size.bit_length() - 1), value & (size - 1)


def dense_kernel(blocks, near, halves, table, tiles_ref, out_ref, held, arrived):
    sections, slots, tile = held.shape[0], held.shape[1], held.shape[-1]
    piece = out_ref.shape[2] // (sections // near)
    copies = [
        pltpu.make_async_copy(tiles_ref.at[section], held.at[section], arrived.at[section])
        for section in range(sections)
    ]
    for copy in copies:
        copy.start()
    out_ref[...] = jnp.zeros_like(out_ref)
    for section, copy in enumerate(copies):
        copy.wait()
        far_place, near_place = split_by(table[section, slots], near)
        for slot in range(slots):
            cell = table[section, slot]

            @pl.when(cell >= 0)
            def _():
                row, column = split_by(cell, blocks)
                half, column = split_by(column, blocks // halves)
                row_at = pl.multiple_of(row * tile, tile)
                column_at = pl.multiple_of(far_place * piece + column * tile, tile)
                out_ref[near_place * halves + half, pl.ds(row_at, tile), pl.ds(column_at, tile)] = held[section, slot]


def dense_blocks(tiles, table, near, halves, blocks):
    sections, _, tile, _ = tiles.shape
    rows = blocks * tile
    shape = (near * halves, rows, sections // near * rows // halves)
    return pl.pallas_call(
        functools.partial(dense_kernel, blocks, near, halves),
        in_specs=[pl.BlockSpec(memory_space=pltpu.SMEM), pl.BlockSpec(memory_space=pltpu.HBM)],
        out_specs=in_vmem(1)[0],
        out_shape=pltpu.VMEM(shape, jnp.bfloat16),
        scratch_shapes=[pltpu.VMEM(tiles.shape, tiles.dtype), pltpu.SemaphoreType.DMA((sections,))],
        compiler_params=params(),
        name="dense_blocks",
    )(table, pltpu.with_memory_space_constraint(tiles, pltpu.HBM))


def lane_of_class():
    return lax.rem(lax.axis_index("blk") + lax.axis_index("rep"), 2)


def unit_at(unit):
    if unit in (0, 3):
        return unit
    return 2 - lane_of_class() if unit == 1 else 1 + lane_of_class()


def aggregate_kernel(spans, based, dense_ref, *refs):
    given, out_ref = refs[:-1], refs[-1]
    total = given[0][...] if based else None
    halves = 2 if lax.axis_size("rep") == 2 and dense_ref.shape[0] > 1 else 1
    for at, first, start, base, size in spans:
        for half in range(halves):
            row = base if halves == 1 else pl.multiple_of(base + (half ^ lax.axis_index("rep")) * size, size)
            term = dot(dense_ref[first + half, :, pl.ds(start, size)], given[based + at][pl.ds(row, size), :])
            total = term if total is None else total + term
    out_ref[...] = total.astype(out_ref.dtype)


def aggregate(dense, spans, parts, base, dtype):
    rows, width = dense.shape[1], parts[0].shape[1]
    given = ([] if base is None else [base]) + parts
    return pl.pallas_call(
        functools.partial(aggregate_kernel, spans, len(given) - len(parts)),
        in_specs=in_vmem(1 + len(given)),
        out_specs=in_vmem(1)[0],
        out_shape=jax.ShapeDtypeStruct((rows, width), dtype),
        compiler_params=params(),
        name="aggregate",
    )(held_in_vmem(dense), *given)


def turn_kernel(share, chunk, own_ref, other_ref, weight_ref, cot_ref, far_cot_ref, dense_ref,
                act_ref, back_ref, sent_ref, g_ref, grad_ref):
    rows = own_ref.shape[0]
    weight = weight_ref[...]
    for half, cot in enumerate((cot_ref, far_cot_ref)):
        at, there = half * share, rows - share - half * share
        g = own_ref[pl.ds(at, share), :].astype(jnp.float32) + other_ref[pl.ds(there, share), :].astype(jnp.float32)
        g = g.astype(jnp.bfloat16)
        value, slope = gelu_and_slope(dot(g, weight))
        grad = (cot[...].astype(jnp.float32) * slope).astype(jnp.bfloat16)
        if half == 0:
            act_ref[...] = value.astype(jnp.bfloat16)
        g_ref[pl.ds(at, share), :] = g
        grad_ref[pl.ds(at, share), :] = grad
        back_ref[:, pl.ds(at, share)] = nt_dot(weight, grad).astype(jnp.bfloat16)
    back = back_ref[...]
    start, size = chunk
    for second in range(2):
        term = dot(back, dense_ref[unit_at(2 + second), :, pl.ds(start, size)])
        sent_ref[:, pl.ds(second * size, size)] = term.astype(jnp.bfloat16)
    part = sent_ref.shape[1] - 2 * size
    columns = pl.ds(pl.multiple_of(lane_of_class() * part, part), part)
    sent_ref[:, pl.ds(2 * size, part)] = tn_dot(g_ref[...], grad_ref[:, columns]).astype(jnp.bfloat16)


def turn(chunk, own, other, weight, cot, far_cot, dense):
    rows, width = own.shape
    share, hid = cot.shape
    bf = jnp.bfloat16
    return pl.pallas_call(
        functools.partial(turn_kernel, share, chunk),
        in_specs=in_vmem(6),
        out_specs=in_vmem(3),
        out_shape=[
            pltpu.VMEM((share, hid), bf),
            jax.ShapeDtypeStruct((width, rows), bf),
            jax.ShapeDtypeStruct((width, 2 * chunk[1] + hid // 2), bf),
        ],
        scratch_shapes=[pltpu.VMEM((rows, width), bf), pltpu.VMEM((rows, hid), bf)],
        compiler_params=params(),
        name="turn",
    )(own, other, weight, cot, far_cot, held_in_vmem(dense))


def rest_kernel(chunks, back_ref, dense_ref, *refs):
    back = back_ref[...]
    for (start, size), sent in zip(chunks, refs[:-1]):
        for second in range(2):
            term = dot(back, dense_ref[unit_at(2 + second), :, pl.ds(start, size)])
            sent[:, pl.ds(second * size, size)] = term.astype(jnp.bfloat16)
    for second in range(2):
        refs[-1][second] = dot(back, dense_ref[unit_at(second)])


def rest_terms(chunks, back, dense):
    width, span = back.shape[0], dense.shape[2]
    return pl.pallas_call(
        functools.partial(rest_kernel, chunks),
        in_specs=in_vmem(2),
        out_specs=in_vmem(len(chunks) + 1),
        out_shape=[jax.ShapeDtypeStruct((width, 2 * size), jnp.bfloat16) for _, size in chunks]
        + [jax.ShapeDtypeStruct((2, width, span), jnp.float32)],
        compiler_params=params(),
        name="rest_terms",
    )(back, held_in_vmem(dense))


def first_sum_kernel(start, size, got_ref, kept_ref, own_ref, sent_ref, total_ref):
    extra = sent_ref.shape[1] - size
    total_ref[...] = kept_ref[0, :, pl.ds(start, size)] + got_ref[:, pl.ds(0, size)].astype(jnp.float32)
    passed = kept_ref[1, :, pl.ds(start, size)] + got_ref[:, pl.ds(size, size)].astype(jnp.float32)
    sent_ref[:, pl.ds(0, size)] = passed.astype(jnp.bfloat16)
    if extra:
        ours = own_ref[:, pl.ds(2 * size, extra)].astype(jnp.float32)
        theirs = got_ref[:, pl.ds(2 * size, extra)].astype(jnp.float32)
        sent_ref[:, pl.ds(size, extra)] = (ours + theirs).astype(jnp.bfloat16)


def first_sum(chunk, got, kept, own):
    width = kept.shape[1]
    start, size = chunk
    extra = got.shape[1] - 2 * size
    return pl.pallas_call(
        functools.partial(first_sum_kernel, start, size),
        in_specs=in_vmem(3),
        out_specs=in_vmem(2),
        out_shape=[
            jax.ShapeDtypeStruct((width, size + extra), jnp.bfloat16),
            jax.ShapeDtypeStruct((width, size), jnp.float32),
        ],
        compiler_params=params(),
        name="first_sum",
    )(got, kept, own)


def second_sum_kernel(got_ref, kept_ref, own_ref, two_ref, three_ref, wg_ref):
    piece = kept_ref.shape[1] // 2
    part = two_ref.shape[1] - piece
    tail = pl.ds(2 * piece, part)
    wg = own_ref[:, tail].astype(jnp.float32) + got_ref[:, tail].astype(jnp.float32)
    wg_ref[...] = wg.astype(jnp.bfloat16)
    for at, out in enumerate((two_ref, three_ref)):
        span = pl.ds(at * piece, piece)
        out[:, pl.ds(0, piece)] = (kept_ref[:, span] + got_ref[:, span].astype(jnp.float32)).astype(jnp.bfloat16)
        out[:, pl.ds(piece, part)] = wg.astype(jnp.bfloat16)


def second_sum(got, kept, own):
    width, size = kept.shape
    message = jax.ShapeDtypeStruct((width, got.shape[1] - size // 2), jnp.bfloat16)
    return pl.pallas_call(
        second_sum_kernel,
        in_specs=in_vmem(3),
        out_specs=in_vmem(3),
        out_shape=[message] * 2 + [jax.ShapeDtypeStruct((width, got.shape[1] - size), jnp.bfloat16)],
        compiler_params=params(),
        name="second_sum",
    )(got, kept, own)


def last_sum_kernel(got_ref, kept_ref, wg_ref, zero_ref, one_ref):
    piece = zero_ref.shape[1]
    tail = pl.ds(piece, one_ref.shape[1] - piece)
    zero_ref[...] = kept_ref[:, pl.ds(0, piece)] + got_ref[:, pl.ds(0, piece)].astype(jnp.float32)
    span = pl.ds(piece, piece)
    one_ref[:, pl.ds(0, piece)] = (kept_ref[:, span] + got_ref[:, span].astype(jnp.float32)).astype(jnp.bfloat16)
    one_ref[:, tail] = wg_ref[...]


def last_sum(got, kept, wg):
    width, size = kept.shape
    return pl.pallas_call(
        last_sum_kernel,
        in_specs=in_vmem(3),
        out_specs=in_vmem(2),
        out_shape=[
            jax.ShapeDtypeStruct((width, size // 2), jnp.float32),
            jax.ShapeDtypeStruct((width, size // 2 + wg.shape[1]), jnp.bfloat16),
        ],
        compiler_params=params(),
        name="last_sum",
    )(got, kept, wg)


def line_sum_kernel(three_ref, two_ref, one_ref, sent_one_ref, zero_ref, out_ref):
    piece = zero_ref.shape[1]
    span, tail = pl.ds(0, piece), pl.ds(piece, out_ref.shape[1] - piece)
    three, two, one = [ref[:, span].astype(jnp.float32) for ref in (three_ref, two_ref, one_ref)]
    out_ref[:, span] = ((zero_ref[...] + one) + (two + three)).astype(jnp.bfloat16)
    three, two, one, own = [ref[:, tail].astype(jnp.float32) for ref in (three_ref, two_ref, one_ref, sent_one_ref)]
    out_ref[:, tail] = ((own + one) + (two + three)).astype(jnp.bfloat16)


def line_sum(three, two, one, sent_one, zero):
    return pl.pallas_call(
        line_sum_kernel,
        in_specs=in_vmem(5),
        out_specs=in_vmem(1)[0],
        out_shape=jax.ShapeDtypeStruct(two.shape, jnp.bfloat16),
        compiler_params=params(),
        name="line_sum",
    )(three, two, one, sent_one, zero)


def finish_kernel(own_ref, got_ref, feat_ref, wg_ref):
    piece = feat_ref.shape[0]
    part = own_ref.shape[1] - piece
    lane = lane_of_class()
    wg_ref[:, pl.ds(pl.multiple_of(lane * part, part), part)] = own_ref[:, pl.ds(piece, part)].astype(jnp.float32)
    wg_ref[:, pl.ds(pl.multiple_of((1 - lane) * part, part), part)] = got_ref[:, pl.ds(piece, part)].astype(jnp.float32)
    span = pl.ds(0, piece)
    ours = jnp.where(lax.axis_index("rep") == 0, own_ref[:, span].astype(jnp.float32), got_ref[:, span].astype(jnp.float32))
    feat_ref[...] = ours.T.astype(jnp.bfloat16)


def finish(own, got, piece):
    width, total = own.shape
    return pl.pallas_call(
        finish_kernel,
        in_specs=in_vmem(2),
        out_specs=in_vmem(2),
        out_shape=[
            jax.ShapeDtypeStruct((piece, width), jnp.bfloat16),
            jax.ShapeDtypeStruct((width, 2 * (total - piece)), jnp.float32),
        ],
        compiler_params=params(),
        name="finish",
    )(own, got)


class Layout:
    def __init__(self, n_blk, reps):
        self.n_blk, self.reps = n_blk, reps

    def route(self, moved):
        pairs = []
        for b in range(self.n_blk):
            for r in range(self.reps):
                to_b, to_r = moved(b, r)
                pairs.append((b * self.reps + r, to_b * self.reps + to_r))
        return pairs

    def owner_to_class(self, mask):
        reps = self.reps
        return self.route(lambda b, r: (((b // reps) ^ mask) * reps + (b + r) % reps, r))

    def class_to_owner(self, mask):
        reps = self.reps
        return self.route(lambda b, r: (((b // reps) ^ mask) * reps + (b - r) % reps, r))

    def in_class(self, mask):
        return self.route(lambda b, r: (b ^ (mask * self.reps), r))

    def along(self, first):
        reps = self.reps

        def moved(b, r):
            lane = (b - r) % reps
            mask, rep_mask = (0, 1) if (lane == 0) == first else (1, 0)
            to_r = r ^ rep_mask
            return (((b // reps) ^ mask) * reps + (lane + to_r) % reps, to_r)

        return self.route(moved)

    def plain(self, mask, rep_mask):
        return self.route(lambda b, r: (b ^ mask, r ^ rep_mask))


def send(value, route):
    return lax.ppermute(value, AXES, route)


def section_table(pos, count, blocks, flip):
    reps, n_blk = lax.axis_size("rep"), lax.axis_size("blk")
    b, r = lax.axis_index("blk"), lax.axis_index("rep")
    sections, slots = pos.shape
    columns = (b - r - jnp.arange(sections, dtype=jnp.int32) * reps) % n_blk
    places = (columns // reps) ^ (b // reps)
    live = jnp.arange(slots, dtype=jnp.int32)[None, :] < count[:, None]
    cells = jnp.where(live, pos ^ (flip * (blocks + 1)), -1)
    return jnp.concatenate([cells, places[:, None]], 1).astype(jnp.int32)


def local_pairs(features, weight, tiles, pos, count, cotangent):
    near, halves = 2, 2
    lay = Layout(lax.axis_size("blk"), lax.axis_size("rep"))
    b, r = lax.axis_index("blk"), lax.axis_index("rep")
    sections, tile = tiles.shape[0], tiles.shape[-1]
    rows, width = features.shape
    blocks, share = rows // tile, rows // halves
    table = section_table(pos, count, blocks, r * (blocks // halves))
    two, one = [send(features, lay.owner_to_class(at * near)) for at in (2, 1)]
    whole, whole_beside = [send(features, lay.owner_to_class(at)) for at in range(2)]
    far_cot = send(cotangent, lay.plain(0, 1))
    three = send(two, lay.in_class(near))
    mine = jnp.concatenate([two, one], 0)
    beside = send(mine, lay.in_class(1))
    beside_three = send(three, lay.in_class(1))
    dense = dense_blocks(tiles, table, near, halves, blocks)
    spans = [(0, 0, 0, 0, share), (1, 2, 0, 0, share), (2, 0, 2 * share, 0, share), (2, 0, share, rows, share),
             (3, 2, 2 * share, 0, share), (3, 2, share, rows, share), (4, 0, 3 * share, 0, share)]
    partial = aggregate(dense, spans, [whole, whole_beside, mine, beside, three], None, jnp.float32)
    partial = aggregate(dense, [(0, 2, 3 * share, 0, share)], [beside_three], partial, jnp.bfloat16)
    other = send(partial, lay.plain(0, 1))
    chunk_a, chunk_b = (2 * share, 2 * share), (0, 2 * share)
    act, back, sent_a = turn(chunk_a, partial, other, weight, cotangent, far_cot, dense)
    got_a = send(sent_a, lay.along(True))
    sent_b, kept = rest_terms([chunk_b], back, dense)
    got_b = send(sent_b, lay.along(True))
    passed_a, kept_a = first_sum(chunk_a, got_a, kept, sent_a)
    back_a = send(passed_a, lay.along(False))
    passed_b, kept_b = first_sum(chunk_b, got_b, kept, sent_b)
    back_b = send(passed_b, lay.along(False))
    sent_two, sent_three, wg = second_sum(back_a, kept_a, passed_a)
    three = send(sent_three, lay.in_class(3 * near))
    two = send(sent_two, lay.in_class(2 * near))
    zero, sent_one = last_sum(back_b, kept_b, wg)
    one = send(sent_one, lay.in_class(near))
    ours = line_sum(three, two, one, sent_one, zero)
    feat_grad, weight_grad = finish(ours, send(ours, lay.plain(1, 0)), share)
    return act, feat_grad, weight_grad


def local_any(features, weight, tiles, pos, count, cotangent):
    reps = lax.axis_size("rep")
    lay = Layout(lax.axis_size("blk"), reps)
    r = lax.axis_index("rep")
    sections, tile = tiles.shape[0], tiles.shape[-1]
    rows = features.shape[0]
    blocks, share = rows // tile, rows // reps
    bf = jnp.bfloat16

    line = jnp.concatenate([send(features, lay.owner_to_class(at)) for at in range(sections)], 0)
    dense = dense_blocks(tiles, section_table(pos, count, blocks, 0), 1, 1, blocks)
    size = line.shape[0]
    partial = aggregate(dense, [(0, 0, 0, 0, size)], [line], None, jnp.float32)
    g = lax.psum(partial, "rep").astype(bf)
    value, slope = gelu_and_slope(dot(g, weight))
    cot = lax.all_gather(cotangent, "rep", axis=0, tiled=True)
    grad = (cot.astype(jnp.float32) * slope).astype(bf)
    act = lax.dynamic_slice_in_dim(value, r * share, share, 0).astype(bf)
    own_g = lax.dynamic_slice_in_dim(g, r * share, share, 0)
    own_grad = lax.dynamic_slice_in_dim(grad, r * share, share, 0)
    weight_grad = lax.psum(tn_dot(own_g, own_grad), AXES)
    back = nt_dot(weight, grad).astype(bf)
    terms = dot(back, dense[0]).astype(bf)
    total = jnp.zeros((back.shape[0], rows), jnp.float32)
    for at in range(sections):
        total += send(terms[:, at * rows:(at + 1) * rows], lay.class_to_owner(at)).astype(jnp.float32)
    feat_grad = lax.psum_scatter(total.T, "rep", scatter_dimension=0, tiled=True).astype(bf)
    return act, feat_grad, weight_grad


def local(features, weight, tile_vals, tile_pos, tile_count, cotangent):
    tiles, pos, count = tile_vals[0, 0], tile_pos[0, 0], tile_count[0, 0]
    reps, tile = lax.axis_size("rep"), tiles.shape[-1]
    paired = reps == 2 and tiles.shape[0] == 8 and features.shape[0] % (2 * tile) == 0
    work = local_pairs if paired else local_any
    return work(features, weight, tiles, pos, count, cotangent)


def solution(mesh):
    placed = (
        P("blk", None),
        P(),
        P("blk", "rep", None, None, None, None),
        P("blk", "rep", None, None),
        P("blk", "rep", None),
        P(("blk", "rep"), None),
    )
    return jax.shard_map(
        local,
        mesh=mesh,
        in_specs=placed,
        out_specs=(P(("blk", "rep"), None), P(("blk", "rep"), None), P()),
        check_vma=False,
    )
```

```python
import functools

import jax
import jax.numpy as jnp
from jax import lax
from jax.experimental import pallas as pl
from jax.experimental.pallas import tpu as pltpu
from jax.sharding import PartitionSpec as P

AXES = ("blk", "rep")
VMEM_LIMIT = 16 * 1024 * 1024


def params():
    return pltpu.CompilerParams(vmem_limit_bytes=VMEM_LIMIT)


def in_vmem(count):
    return [pl.BlockSpec(memory_space=pltpu.VMEM)] * count


def held_in_vmem(value):
    return pltpu.with_memory_space_constraint(value, pltpu.VMEM)


def gelu_and_slope(v):
    scale = 0.7978845608028654
    square = v * v
    t = jnp.tanh(scale * (v + 0.044715 * (square * v)))
    half = 0.5 * (1.0 + t)
    slope = half + (0.5 * scale) * v * (1.0 - t * t) * (1.0 + 3.0 * 0.044715 * square)
    return v * half, slope


def nt_dot(a, b):
    return lax.dot_general(a, b, (((1,), (1,)), ((), ())), preferred_element_type=jnp.float32)


def tn_dot(a, b):
    return lax.dot_general(a, b, (((0,), (0,)), ((), ())), preferred_element_type=jnp.float32)


def dot(a, b):
    return jnp.dot(a, b, preferred_element_type=jnp.float32)


def split_by(value, size):
    if size & (size - 1):
        return lax.div(value, size), lax.rem(value, size)
    return lax.shift_right_logical(value, size.bit_length() - 1), value & (size - 1)


def dense_kernel(blocks, near, halves, table, tiles_ref, out_ref, held, arrived):
    sections, slots, tile = held.shape[0], held.shape[1], held.shape[-1]
    piece = out_ref.shape[2] // (sections // near)
    copies = [
        pltpu.make_async_copy(tiles_ref.at[section], held.at[section], arrived.at[section])
        for section in range(sections)
    ]
    for copy in copies:
        copy.start()
    out_ref[...] = jnp.zeros_like(out_ref)
    for section, copy in enumerate(copies):
        copy.wait()
        far_place, near_place = split_by(table[section, slots], near)
        for slot in range(slots):
            cell = table[section, slot]

            @pl.when(cell >= 0)
            def _():
                row, column = split_by(cell, blocks)
                half, column = split_by(column, blocks // halves)
                row_at = pl.multiple_of(row * tile, tile)
                column_at = pl.multiple_of(far_place * piece + column * tile, tile)
                out_ref[near_place * halves + half, pl.ds(row_at, tile), pl.ds(column_at, tile)] = held[section, slot]


def dense_blocks(tiles, table, near, halves, blocks):
    sections, _, tile, _ = tiles.shape
    rows = blocks * tile
    shape = (near * halves, rows, sections // near * rows // halves)
    return pl.pallas_call(
        functools.partial(dense_kernel, blocks, near, halves),
        in_specs=[pl.BlockSpec(memory_space=pltpu.SMEM), pl.BlockSpec(memory_space=pltpu.HBM)],
        out_specs=in_vmem(1)[0],
        out_shape=pltpu.VMEM(shape, jnp.bfloat16),
        scratch_shapes=[pltpu.VMEM(tiles.shape, tiles.dtype), pltpu.SemaphoreType.DMA((sections,))],
        compiler_params=params(),
        name="dense_blocks",
    )(table, pltpu.with_memory_space_constraint(tiles, pltpu.HBM))


def lane_of_class():
    return lax.rem(lax.axis_index("blk") + lax.axis_index("rep"), 2)


def unit_at(unit):
    if unit in (0, 3):
        return unit
    return 2 - lane_of_class() if unit == 1 else 1 + lane_of_class()


def aggregate_kernel(spans, based, dense_ref, *refs):
    given, out_ref = refs[:-1], refs[-1]
    total = given[0][...] if based else None
    halves = 2 if lax.axis_size("rep") == 2 and dense_ref.shape[0] > 1 else 1
    for at, first, start, base, size in spans:
        for half in range(halves):
            row = base if halves == 1 else pl.multiple_of(base + (half ^ lax.axis_index("rep")) * size, size)
            term = dot(dense_ref[first + half, :, pl.ds(start, size)], given[based + at][pl.ds(row, size), :])
            total = term if total is None else total + term
    out_ref[...] = total.astype(out_ref.dtype)


def aggregate(dense, spans, parts, base, dtype):
    rows, width = dense.shape[1], parts[0].shape[1]
    given = ([] if base is None else [base]) + parts
    return pl.pallas_call(
        functools.partial(aggregate_kernel, spans, len(given) - len(parts)),
        in_specs=in_vmem(1 + len(given)),
        out_specs=in_vmem(1)[0],
        out_shape=jax.ShapeDtypeStruct((rows, width), dtype),
        compiler_params=params(),
        name="aggregate",
    )(held_in_vmem(dense), *given)


def turn_kernel(share, chunk, own_ref, other_ref, weight_ref, cot_ref, far_cot_ref, dense_ref,
                act_ref, back_ref, sent_ref, wg_ref, g_ref, grad_ref):
    rows = own_ref.shape[0]
    weight = weight_ref[...]
    for half, cot in enumerate((cot_ref, far_cot_ref)):
        at, there = half * share, rows - share - half * share
        g = own_ref[pl.ds(at, share), :].astype(jnp.float32) + other_ref[pl.ds(there, share), :].astype(jnp.float32)
        g = g.astype(jnp.bfloat16)
        value, slope = gelu_and_slope(dot(g, weight))
        grad = (cot[...].astype(jnp.float32) * slope).astype(jnp.bfloat16)
        if half == 0:
            act_ref[...] = value.astype(jnp.bfloat16)
        g_ref[pl.ds(at, share), :] = g
        grad_ref[pl.ds(at, share), :] = grad
        back_ref[:, pl.ds(at, share)] = nt_dot(weight, grad).astype(jnp.bfloat16)
    back = back_ref[...]
    start, size = chunk
    for second in range(2):
        term = dot(back, dense_ref[unit_at(2 + second), :, pl.ds(start, size)])
        sent_ref[:, pl.ds(second * size, size)] = term.astype(jnp.bfloat16)
    part = wg_ref.shape[1]
    columns = pl.ds(pl.multiple_of(lane_of_class() * part, part), part)
    wg_ref[...] = tn_dot(g_ref[...], grad_ref[:, columns]).astype(jnp.bfloat16)


def turn(chunk, own, other, weight, cot, far_cot, dense):
    rows, width = own.shape
    share, hid = cot.shape
    bf = jnp.bfloat16
    return pl.pallas_call(
        functools.partial(turn_kernel, share, chunk),
        in_specs=in_vmem(6),
        out_specs=in_vmem(4),
        out_shape=[
            pltpu.VMEM((share, hid), bf),
            jax.ShapeDtypeStruct((width, rows), bf),
            jax.ShapeDtypeStruct((width, 2 * chunk[1]), bf),
            jax.ShapeDtypeStruct((width, hid // 2), bf),
        ],
        scratch_shapes=[pltpu.VMEM((rows, width), bf), pltpu.VMEM((rows, hid), bf)],
        compiler_params=params(),
        name="turn",
    )(own, other, weight, cot, far_cot, held_in_vmem(dense))


def rest_kernel(chunks, back_ref, dense_ref, *refs):
    back = back_ref[...]
    for (start, size), sent in zip(chunks, refs[:-1]):
        for second in range(2):
            term = dot(back, dense_ref[unit_at(2 + second), :, pl.ds(start, size)])
            sent[:, pl.ds(second * size, size)] = term.astype(jnp.bfloat16)
    for second in range(2):
        refs[-1][second] = dot(back, dense_ref[unit_at(second)])


def rest_terms(chunks, back, dense):
    width, span = back.shape[0], dense.shape[2]
    return pl.pallas_call(
        functools.partial(rest_kernel, chunks),
        in_specs=in_vmem(2),
        out_specs=in_vmem(len(chunks) + 1),
        out_shape=[jax.ShapeDtypeStruct((width, 2 * size), jnp.bfloat16) for _, size in chunks]
        + [jax.ShapeDtypeStruct((2, width, span), jnp.float32)],
        compiler_params=params(),
        name="rest_terms",
    )(back, held_in_vmem(dense))


def first_sum_kernel(start, size, got_ref, kept_ref, after_ref, sent_ref, total_ref, mark_ref):
    total_ref[...] = kept_ref[0, :, pl.ds(start, size)] + got_ref[:, pl.ds(0, size)].astype(jnp.float32)
    passed = kept_ref[1, :, pl.ds(start, size)] + got_ref[:, pl.ds(size, size)].astype(jnp.float32)
    sent_ref[...] = passed.astype(jnp.bfloat16)
    mark_ref[...] = jnp.zeros_like(mark_ref)


MARK = jax.ShapeDtypeStruct((16, 128), jnp.bfloat16)


def first_sum(chunk, got, kept, after):
    width = kept.shape[1]
    start, size = chunk
    return pl.pallas_call(
        functools.partial(first_sum_kernel, start, size),
        in_specs=in_vmem(3),
        out_specs=in_vmem(3),
        out_shape=[
            jax.ShapeDtypeStruct((width, size), jnp.bfloat16),
            jax.ShapeDtypeStruct((width, size), jnp.float32),
            MARK,
        ],
        compiler_params=params(),
        name="first_sum",
    )(got, kept, after)


def second_sum_kernel(got_ref, kept_ref, after_ref, first_ref, second_ref, mark_ref):
    piece = kept_ref.shape[1] // 2
    for at, out in enumerate((first_ref, second_ref)):
        span = pl.ds(at * piece, piece)
        out[...] = (kept_ref[:, span] + got_ref[:, span].astype(jnp.float32)).astype(out.dtype)
    mark_ref[...] = jnp.zeros_like(mark_ref)


def second_sum(got, kept, first_type, after):
    width, size = kept.shape
    return pl.pallas_call(
        second_sum_kernel,
        in_specs=in_vmem(3),
        out_specs=in_vmem(3),
        out_shape=[jax.ShapeDtypeStruct((width, size // 2), kind) for kind in (first_type, jnp.bfloat16)] + [MARK],
        compiler_params=params(),
        name="second_sum",
    )(got, kept, after)


def add_kernel(a_ref, b_ref, after_ref, out_ref):
    out_ref[...] = (a_ref[...].astype(jnp.float32) + b_ref[...].astype(jnp.float32)).astype(out_ref.dtype)


def add(a, b, after):
    return pl.pallas_call(
        add_kernel,
        in_specs=in_vmem(3),
        out_specs=in_vmem(1)[0],
        out_shape=jax.ShapeDtypeStruct(a.shape, a.dtype),
        compiler_params=params(),
        name="add",
    )(a, b, after)


def line_sum_kernel(three_ref, two_ref, one_ref, zero_ref, wg_ref, got_wg_ref, out_ref):
    piece = zero_ref.shape[1]
    span, tail = pl.ds(0, piece), pl.ds(piece, out_ref.shape[1] - piece)
    three, two, one = [ref[...].astype(jnp.float32) for ref in (three_ref, two_ref, one_ref)]
    out_ref[:, span] = ((zero_ref[...] + one) + (two + three)).astype(jnp.bfloat16)
    out_ref[:, tail] = (wg_ref[...].astype(jnp.float32) + got_wg_ref[...].astype(jnp.float32)).astype(jnp.bfloat16)


def line_sum(three, two, one, zero, wg, got_wg):
    width, piece = zero.shape
    return pl.pallas_call(
        line_sum_kernel,
        in_specs=in_vmem(6),
        out_specs=in_vmem(1)[0],
        out_shape=jax.ShapeDtypeStruct((width, piece + wg.shape[1]), jnp.bfloat16),
        compiler_params=params(),
        name="line_sum",
    )(three, two, one, zero, wg, got_wg)


def finish_kernel(own_ref, got_ref, feat_ref, wg_ref):
    piece = feat_ref.shape[0]
    part = own_ref.shape[1] - piece
    lane = lane_of_class()
    wg_ref[:, pl.ds(pl.multiple_of(lane * part, part), part)] = own_ref[:, pl.ds(piece, part)].astype(jnp.float32)
    wg_ref[:, pl.ds(pl.multiple_of((1 - lane) * part, part), part)] = got_ref[:, pl.ds(piece, part)].astype(jnp.float32)
    span = pl.ds(0, piece)
    ours = jnp.where(lax.axis_index("rep") == 0, own_ref[:, span].astype(jnp.float32), got_ref[:, span].astype(jnp.float32))
    feat_ref[...] = ours.T.astype(jnp.bfloat16)


def finish(own, got, piece):
    width, total = own.shape
    return pl.pallas_call(
        finish_kernel,
        in_specs=in_vmem(2),
        out_specs=in_vmem(2),
        out_shape=[
            jax.ShapeDtypeStruct((piece, width), jnp.bfloat16),
            jax.ShapeDtypeStruct((width, 2 * (total - piece)), jnp.float32),
        ],
        compiler_params=params(),
        name="finish",
    )(own, got)


class Layout:
    def __init__(self, n_blk, reps):
        self.n_blk, self.reps = n_blk, reps

    def route(self, moved):
        pairs = []
        for b in range(self.n_blk):
            for r in range(self.reps):
                to_b, to_r = moved(b, r)
                pairs.append((b * self.reps + r, to_b * self.reps + to_r))
        return pairs

    def owner_to_class(self, mask):
        reps = self.reps
        return self.route(lambda b, r: (((b // reps) ^ mask) * reps + (b + r) % reps, r))

    def class_to_owner(self, mask):
        reps = self.reps
        return self.route(lambda b, r: (((b // reps) ^ mask) * reps + (b - r) % reps, r))

    def in_class(self, mask):
        return self.route(lambda b, r: (b ^ (mask * self.reps), r))

    def along(self, first):
        reps = self.reps

        def moved(b, r):
            lane = (b - r) % reps
            mask, rep_mask = (0, 1) if (lane == 0) == first else (1, 0)
            to_r = r ^ rep_mask
            return (((b // reps) ^ mask) * reps + (lane + to_r) % reps, to_r)

        return self.route(moved)

    def plain(self, mask, rep_mask):
        return self.route(lambda b, r: (b ^ mask, r ^ rep_mask))


def send(value, route):
    return lax.ppermute(value, AXES, route)


def section_table(pos, count, blocks, flip):
    reps, n_blk = lax.axis_size("rep"), lax.axis_size("blk")
    b, r = lax.axis_index("blk"), lax.axis_index("rep")
    sections, slots = pos.shape
    columns = (b - r - jnp.arange(sections, dtype=jnp.int32) * reps) % n_blk
    places = (columns // reps) ^ (b // reps)
    live = jnp.arange(slots, dtype=jnp.int32)[None, :] < count[:, None]
    cells = jnp.where(live, pos ^ (flip * (blocks + 1)), -1)
    return jnp.concatenate([cells, places[:, None]], 1).astype(jnp.int32)


def local_pairs(features, weight, tiles, pos, count, cotangent):
    near, halves = 2, 2
    lay = Layout(lax.axis_size("blk"), lax.axis_size("rep"))
    b, r = lax.axis_index("blk"), lax.axis_index("rep")
    sections, tile = tiles.shape[0], tiles.shape[-1]
    rows, width = features.shape
    blocks, share = rows // tile, rows // halves
    table = section_table(pos, count, blocks, r * (blocks // halves))
    two, one = [send(features, lay.owner_to_class(at * near)) for at in (2, 1)]
    whole, whole_beside = [send(features, lay.owner_to_class(at)) for at in range(2)]
    far_cot = send(cotangent, lay.plain(0, 1))
    three = send(two, lay.in_class(near))
    mine = jnp.concatenate([two, one], 0)
    beside = send(mine, lay.in_class(1))
    beside_three = send(three, lay.in_class(1))
    dense = dense_blocks(tiles, table, near, halves, blocks)
    spans = [(0, 0, 0, 0, share), (1, 2, 0, 0, share), (2, 0, 2 * share, 0, share), (2, 0, share, rows, share),
             (3, 2, 2 * share, 0, share), (3, 2, share, rows, share), (4, 0, 3 * share, 0, share)]
    partial = aggregate(dense, spans, [whole, whole_beside, mine, beside, three], None, jnp.float32)
    partial = aggregate(dense, [(0, 2, 3 * share, 0, share)], [beside_three], partial, jnp.bfloat16)
    other = send(partial, lay.plain(0, 1))
    chunk_a, chunk_b = (2 * share, 2 * share), (0, 2 * share)
    act, back, sent_a, wg = turn(chunk_a, partial, other, weight, cotangent, far_cot, dense)
    got_a = send(sent_a, lay.along(True))
    sent_b, kept = rest_terms([chunk_b], back, dense)
    got_b = send(sent_b, lay.along(True))
    got_w1 = send(wg, lay.in_class(2 * near))
    passed_a, kept_a, mark_a = first_sum(chunk_a, got_a, kept, got_w1)
    back_a = send(passed_a, lay.along(False))
    passed_b, kept_b, mark_b = first_sum(chunk_b, got_b, kept, mark_a)
    back_b = send(passed_b, lay.along(False))
    wg = add(wg, got_w1, mark_b)
    got_w2 = send(wg, lay.in_class(near))
    two, three, mark_c = second_sum(back_a, kept_a, jnp.bfloat16, back)
    three = send(three, lay.in_class(3 * near))
    two = send(two, lay.in_class(2 * near))
    zero, one, mark_d = second_sum(back_b, kept_b, jnp.float32, mark_c)
    one = send(one, lay.in_class(near))
    wg = add(wg, got_w2, mark_c)
    wg = add(wg, send(wg, lay.along(True)), mark_d)
    ours = line_sum(three, two, one, zero, wg, send(wg, lay.along(False)))
    feat_grad, weight_grad = finish(ours, send(ours, lay.plain(1, 0)), share)
    return act, feat_grad, weight_grad


def local_any(features, weight, tiles, pos, count, cotangent):
    reps = lax.axis_size("rep")
    lay = Layout(lax.axis_size("blk"), reps)
    r = lax.axis_index("rep")
    sections, tile = tiles.shape[0], tiles.shape[-1]
    rows = features.shape[0]
    blocks, share = rows // tile, rows // reps
    bf = jnp.bfloat16

    line = jnp.concatenate([send(features, lay.owner_to_class(at)) for at in range(sections)], 0)
    dense = dense_blocks(tiles, section_table(pos, count, blocks, 0), 1, 1, blocks)
    size = line.shape[0]
    partial = aggregate(dense, [(0, 0, 0, 0, size)], [line], None, jnp.float32)
    g = lax.psum(partial, "rep").astype(bf)
    value, slope = gelu_and_slope(dot(g, weight))
    cot = lax.all_gather(cotangent, "rep", axis=0, tiled=True)
    grad = (cot.astype(jnp.float32) * slope).astype(bf)
    act = lax.dynamic_slice_in_dim(value, r * share, share, 0).astype(bf)
    own_g = lax.dynamic_slice_in_dim(g, r * share, share, 0)
    own_grad = lax.dynamic_slice_in_dim(grad, r * share, share, 0)
    weight_grad = lax.psum(tn_dot(own_g, own_grad), AXES)
    back = nt_dot(weight, grad).astype(bf)
    terms = dot(back, dense[0]).astype(bf)
    total = jnp.zeros((back.shape[0], rows), jnp.float32)
    for at in range(sections):
        total += send(terms[:, at * rows:(at + 1) * rows], lay.class_to_owner(at)).astype(jnp.float32)
    feat_grad = lax.psum_scatter(total.T, "rep", scatter_dimension=0, tiled=True).astype(bf)
    return act, feat_grad, weight_grad


def local(features, weight, tile_vals, tile_pos, tile_count, cotangent):
    tiles, pos, count = tile_vals[0, 0], tile_pos[0, 0], tile_count[0, 0]
    reps, tile = lax.axis_size("rep"), tiles.shape[-1]
    paired = reps == 2 and tiles.shape[0] == 8 and features.shape[0] % (2 * tile) == 0
    work = local_pairs if paired else local_any
    return work(features, weight, tiles, pos, count, cotangent)


def solution(mesh):
    placed = (
        P("blk", None),
        P(),
        P("blk", "rep", None, None, None, None),
        P("blk", "rep", None, None),
        P("blk", "rep", None),
        P(("blk", "rep"), None),
    )
    return jax.shard_map(
        local,
        mesh=mesh,
        in_specs=placed,
        out_specs=(P(("blk", "rep"), None), P(("blk", "rep"), None), P()),
        check_vma=False,
    )
```

```python
import functools

import jax
import jax.numpy as jnp
from jax import lax
from jax.experimental import pallas as pl
from jax.experimental.pallas import tpu as pltpu
from jax.sharding import PartitionSpec as P

AXES = ("blk", "rep")
VMEM_LIMIT = 16 * 1024 * 1024


def params():
    return pltpu.CompilerParams(vmem_limit_bytes=VMEM_LIMIT)


def in_vmem(count):
    return [pl.BlockSpec(memory_space=pltpu.VMEM)] * count


def held_in_vmem(value):
    return pltpu.with_memory_space_constraint(value, pltpu.VMEM)


def gelu_and_slope(v):
    scale = 0.7978845608028654
    square = v * v
    t = jnp.tanh(scale * (v + 0.044715 * (square * v)))
    half = 0.5 * (1.0 + t)
    slope = half + (0.5 * scale) * v * (1.0 - t * t) * (1.0 + 3.0 * 0.044715 * square)
    return v * half, slope


def nt_dot(a, b):
    return lax.dot_general(a, b, (((1,), (1,)), ((), ())), preferred_element_type=jnp.float32)


def tn_dot(a, b):
    return lax.dot_general(a, b, (((0,), (0,)), ((), ())), preferred_element_type=jnp.float32)


def dot(a, b):
    return jnp.dot(a, b, preferred_element_type=jnp.float32)


def split_by(value, size):
    if size & (size - 1):
        return lax.div(value, size), lax.rem(value, size)
    return lax.shift_right_logical(value, size.bit_length() - 1), value & (size - 1)


def dense_kernel(blocks, near, halves, table, tiles_ref, out_ref, held, arrived):
    sections, slots, tile = held.shape[0], held.shape[1], held.shape[-1]
    piece = out_ref.shape[2] // (sections // near)
    copies = [
        pltpu.make_async_copy(tiles_ref.at[section], held.at[section], arrived.at[section])
        for section in range(sections)
    ]
    for copy in copies:
        copy.start()
    out_ref[...] = jnp.zeros_like(out_ref)
    for section, copy in enumerate(copies):
        copy.wait()
        far_place, near_place = split_by(table[section, slots], near)
        for slot in range(slots):
            cell = table[section, slot]

            @pl.when(cell >= 0)
            def _():
                row, column = split_by(cell, blocks)
                half, column = split_by(column, blocks // halves)
                row_at = pl.multiple_of(row * tile, tile)
                column_at = pl.multiple_of(far_place * piece + column * tile, tile)
                out_ref[near_place * halves + half, pl.ds(row_at, tile), pl.ds(column_at, tile)] = held[section, slot]


def dense_blocks(tiles, table, near, halves, blocks):
    sections, _, tile, _ = tiles.shape
    rows = blocks * tile
    shape = (near * halves, rows, sections // near * rows // halves)
    return pl.pallas_call(
        functools.partial(dense_kernel, blocks, near, halves),
        in_specs=[pl.BlockSpec(memory_space=pltpu.SMEM), pl.BlockSpec(memory_space=pltpu.HBM)],
        out_specs=in_vmem(1)[0],
        out_shape=pltpu.VMEM(shape, jnp.bfloat16),
        scratch_shapes=[pltpu.VMEM(tiles.shape, tiles.dtype), pltpu.SemaphoreType.DMA((sections,))],
        compiler_params=params(),
        name="dense_blocks",
    )(table, pltpu.with_memory_space_constraint(tiles, pltpu.HBM))


def lane_of_class():
    return lax.rem(lax.axis_index("blk") + lax.axis_index("rep"), 2)


def unit_at(unit):
    if unit in (0, 3):
        return unit
    return 2 - lane_of_class() if unit == 1 else 1 + lane_of_class()


def aggregate_kernel(spans, based, dense_ref, *refs):
    given, out_ref = refs[:-1], refs[-1]
    total = given[0][...] if based else None
    halves = 2 if lax.axis_size("rep") == 2 and dense_ref.shape[0] > 1 else 1
    for at, first, start, base, size in spans:
        for half in range(halves):
            row = base if halves == 1 else pl.multiple_of(base + (half ^ lax.axis_index("rep")) * size, size)
            term = dot(dense_ref[first + half, :, pl.ds(start, size)], given[based + at][pl.ds(row, size), :])
            total = term if total is None else total + term
    out_ref[...] = total.astype(out_ref.dtype)


def aggregate(dense, spans, parts, base, dtype):
    rows, width = dense.shape[1], parts[0].shape[1]
    given = ([] if base is None else [base]) + parts
    return pl.pallas_call(
        functools.partial(aggregate_kernel, spans, len(given) - len(parts)),
        in_specs=in_vmem(1 + len(given)),
        out_specs=in_vmem(1)[0],
        out_shape=jax.ShapeDtypeStruct((rows, width), dtype),
        compiler_params=params(),
        name="aggregate",
    )(held_in_vmem(dense), *given)


def turn_kernel(share, chunk, own_ref, other_ref, weight_ref, cot_ref, far_cot_ref, dense_ref,
                act_ref, back_ref, sent_ref, wg_ref, g_ref, grad_ref):
    rows = own_ref.shape[0]
    weight = weight_ref[...]
    for half, cot in enumerate((cot_ref, far_cot_ref)):
        at, there = half * share, rows - share - half * share
        g = own_ref[pl.ds(at, share), :].astype(jnp.float32) + other_ref[pl.ds(there, share), :].astype(jnp.float32)
        g = g.astype(jnp.bfloat16)
        value, slope = gelu_and_slope(dot(g, weight))
        grad = (cot[...].astype(jnp.float32) * slope).astype(jnp.bfloat16)
        if half == 0:
            act_ref[...] = value.astype(jnp.bfloat16)
        g_ref[pl.ds(at, share), :] = g
        grad_ref[pl.ds(at, share), :] = grad
        back_ref[:, pl.ds(at, share)] = nt_dot(weight, grad).astype(jnp.bfloat16)
    back = back_ref[...]
    start, size = chunk
    for second in range(2):
        term = dot(back, dense_ref[unit_at(2 + second), :, pl.ds(start, size)])
        sent_ref[:, pl.ds(second * size, size)] = term.astype(jnp.bfloat16)
    part = wg_ref.shape[1]
    columns = pl.ds(pl.multiple_of(lane_of_class() * part, part), part)
    wg_ref[...] = tn_dot(g_ref[...], grad_ref[:, columns]).astype(jnp.bfloat16)


def turn(chunk, own, other, weight, cot, far_cot, dense):
    rows, width = own.shape
    share, hid = cot.shape
    bf = jnp.bfloat16
    return pl.pallas_call(
        functools.partial(turn_kernel, share, chunk),
        in_specs=in_vmem(6),
        out_specs=in_vmem(4),
        out_shape=[
            pltpu.VMEM((share, hid), bf),
            jax.ShapeDtypeStruct((width, rows), bf),
            jax.ShapeDtypeStruct((width, 2 * chunk[1]), bf),
            jax.ShapeDtypeStruct((width, hid // 2), bf),
        ],
        scratch_shapes=[pltpu.VMEM((rows, width), bf), pltpu.VMEM((rows, hid), bf)],
        compiler_params=params(),
        name="turn",
    )(own, other, weight, cot, far_cot, held_in_vmem(dense))


def rest_kernel(chunks, back_ref, dense_ref, *refs):
    back = back_ref[...]
    for (start, size), sent in zip(chunks, refs[:-1]):
        for second in range(2):
            term = dot(back, dense_ref[unit_at(2 + second), :, pl.ds(start, size)])
            sent[:, pl.ds(second * size, size)] = term.astype(jnp.bfloat16)
    for second in range(2):
        refs[-1][second] = dot(back, dense_ref[unit_at(second)])


def rest_terms(chunks, back, dense):
    width, span = back.shape[0], dense.shape[2]
    return pl.pallas_call(
        functools.partial(rest_kernel, chunks),
        in_specs=in_vmem(2),
        out_specs=in_vmem(len(chunks) + 1),
        out_shape=[jax.ShapeDtypeStruct((width, 2 * size), jnp.bfloat16) for _, size in chunks]
        + [jax.ShapeDtypeStruct((2, width, span), jnp.float32)],
        compiler_params=params(),
        name="rest_terms",
    )(back, held_in_vmem(dense))


def first_sum_kernel(start, size, got_ref, kept_ref, after_ref, sent_ref, total_ref, mark_ref):
    total_ref[...] = kept_ref[0, :, pl.ds(start, size)] + got_ref[:, pl.ds(0, size)].astype(jnp.float32)
    passed = kept_ref[1, :, pl.ds(start, size)] + got_ref[:, pl.ds(size, size)].astype(jnp.float32)
    sent_ref[...] = passed.astype(jnp.bfloat16)
    mark_ref[...] = jnp.zeros_like(mark_ref)


MARK = jax.ShapeDtypeStruct((16, 128), jnp.bfloat16)


def first_sum(chunk, got, kept, after):
    width = kept.shape[1]
    start, size = chunk
    return pl.pallas_call(
        functools.partial(first_sum_kernel, start, size),
        in_specs=in_vmem(3),
        out_specs=in_vmem(3),
        out_shape=[
            jax.ShapeDtypeStruct((width, size), jnp.bfloat16),
            jax.ShapeDtypeStruct((width, size), jnp.float32),
            MARK,
        ],
        compiler_params=params(),
        name="first_sum",
    )(got, kept, after)


def second_sum_kernel(got_ref, kept_ref, after_ref, first_ref, second_ref, mark_ref):
    piece = kept_ref.shape[1] // 2
    for at, out in enumerate((first_ref, second_ref)):
        span = pl.ds(at * piece, piece)
        out[...] = (kept_ref[:, span] + got_ref[:, span].astype(jnp.float32)).astype(out.dtype)
    mark_ref[...] = jnp.zeros_like(mark_ref)


def second_sum(got, kept, first_type, after):
    width, size = kept.shape
    return pl.pallas_call(
        second_sum_kernel,
        in_specs=in_vmem(3),
        out_specs=in_vmem(3),
        out_shape=[jax.ShapeDtypeStruct((width, size // 2), kind) for kind in (first_type, jnp.bfloat16)] + [MARK],
        compiler_params=params(),
        name="second_sum",
    )(got, kept, after)


def add_kernel(a_ref, b_ref, after_ref, out_ref):
    out_ref[...] = (a_ref[...].astype(jnp.float32) + b_ref[...].astype(jnp.float32)).astype(out_ref.dtype)


def add(a, b, after):
    return pl.pallas_call(
        add_kernel,
        in_specs=in_vmem(3),
        out_specs=in_vmem(1)[0],
        out_shape=jax.ShapeDtypeStruct(a.shape, a.dtype),
        compiler_params=params(),
        name="add",
    )(a, b, after)


def line_sum_kernel(three_ref, two_ref, one_ref, zero_ref, wg_ref, got_wg_ref, out_ref):
    piece = zero_ref.shape[1]
    span, tail = pl.ds(0, piece), pl.ds(piece, out_ref.shape[1] - piece)
    three, two, one = [ref[...].astype(jnp.float32) for ref in (three_ref, two_ref, one_ref)]
    out_ref[:, span] = ((zero_ref[...] + one) + (two + three)).astype(jnp.bfloat16)
    out_ref[:, tail] = (wg_ref[...].astype(jnp.float32) + got_wg_ref[...].astype(jnp.float32)).astype(jnp.bfloat16)


def line_sum(three, two, one, zero, wg, got_wg):
    width, piece = zero.shape
    return pl.pallas_call(
        line_sum_kernel,
        in_specs=in_vmem(6),
        out_specs=in_vmem(1)[0],
        out_shape=jax.ShapeDtypeStruct((width, piece + wg.shape[1]), jnp.bfloat16),
        compiler_params=params(),
        name="line_sum",
    )(three, two, one, zero, wg, got_wg)


def finish_kernel(own_ref, got_ref, feat_ref, wg_ref):
    piece = feat_ref.shape[0]
    part = own_ref.shape[1] - piece
    lane = lane_of_class()
    wg_ref[:, pl.ds(pl.multiple_of(lane * part, part), part)] = own_ref[:, pl.ds(piece, part)].astype(jnp.float32)
    wg_ref[:, pl.ds(pl.multiple_of((1 - lane) * part, part), part)] = got_ref[:, pl.ds(piece, part)].astype(jnp.float32)
    span = pl.ds(0, piece)
    ours = jnp.where(lax.axis_index("rep") == 0, own_ref[:, span].astype(jnp.float32), got_ref[:, span].astype(jnp.float32))
    feat_ref[...] = ours.T.astype(jnp.bfloat16)


def finish(own, got, piece):
    width, total = own.shape
    return pl.pallas_call(
        finish_kernel,
        in_specs=in_vmem(2),
        out_specs=in_vmem(2),
        out_shape=[
            jax.ShapeDtypeStruct((piece, width), jnp.bfloat16),
            jax.ShapeDtypeStruct((width, 2 * (total - piece)), jnp.float32),
        ],
        compiler_params=params(),
        name="finish",
    )(own, got)


class Layout:
    def __init__(self, n_blk, reps):
        self.n_blk, self.reps = n_blk, reps

    def route(self, moved):
        pairs = []
        for b in range(self.n_blk):
            for r in range(self.reps):
                to_b, to_r = moved(b, r)
                pairs.append((b * self.reps + r, to_b * self.reps + to_r))
        return pairs

    def owner_to_class(self, mask):
        reps = self.reps
        return self.route(lambda b, r: (((b // reps) ^ mask) * reps + (b + r) % reps, r))

    def class_to_owner(self, mask):
        reps = self.reps
        return self.route(lambda b, r: (((b // reps) ^ mask) * reps + (b - r) % reps, r))

    def in_class(self, mask):
        return self.route(lambda b, r: (b ^ (mask * self.reps), r))

    def along(self, first):
        reps = self.reps

        def moved(b, r):
            lane = (b - r) % reps
            mask, rep_mask = (0, 1) if (lane == 0) == first else (1, 0)
            to_r = r ^ rep_mask
            return (((b // reps) ^ mask) * reps + (lane + to_r) % reps, to_r)

        return self.route(moved)

    def plain(self, mask, rep_mask):
        return self.route(lambda b, r: (b ^ mask, r ^ rep_mask))


def send(value, route):
    return lax.ppermute(value, AXES, route)


def section_table(pos, count, blocks, flip):
    reps, n_blk = lax.axis_size("rep"), lax.axis_size("blk")
    b, r = lax.axis_index("blk"), lax.axis_index("rep")
    sections, slots = pos.shape
    columns = (b - r - jnp.arange(sections, dtype=jnp.int32) * reps) % n_blk
    places = (columns // reps) ^ (b // reps)
    live = jnp.arange(slots, dtype=jnp.int32)[None, :] < count[:, None]
    cells = jnp.where(live, pos ^ (flip * (blocks + 1)), -1)
    return jnp.concatenate([cells, places[:, None]], 1).astype(jnp.int32)


def local_pairs(features, weight, tiles, pos, count, cotangent):
    near, halves = 2, 2
    lay = Layout(lax.axis_size("blk"), lax.axis_size("rep"))
    b, r = lax.axis_index("blk"), lax.axis_index("rep")
    sections, tile = tiles.shape[0], tiles.shape[-1]
    rows, width = features.shape
    blocks, share = rows // tile, rows // halves
    table = section_table(pos, count, blocks, r * (blocks // halves))
    two, one = [send(features, lay.owner_to_class(at * near)) for at in (2, 1)]
    whole, whole_beside = [send(features, lay.owner_to_class(at)) for at in range(2)]
    far_cot = send(cotangent, lay.plain(0, 1))
    three = send(two, lay.in_class(near))
    mine = jnp.concatenate([two, one], 0)
    beside = send(mine, lay.in_class(1))
    beside_three = send(three, lay.in_class(1))
    dense = dense_blocks(tiles, table, near, halves, blocks)
    spans = [(0, 0, 0, 0, share), (1, 2, 0, 0, share), (2, 0, 2 * share, 0, share), (2, 0, share, rows, share),
             (3, 2, 2 * share, 0, share), (3, 2, share, rows, share), (4, 0, 3 * share, 0, share)]
    partial = aggregate(dense, spans, [whole, whole_beside, mine, beside, three], None, jnp.float32)
    partial = aggregate(dense, [(0, 2, 3 * share, 0, share)], [beside_three], partial, jnp.bfloat16)
    other = send(partial, lay.plain(0, 1))
    chunk_a, chunk_b = (2 * share, 2 * share), (0, 2 * share)
    act, back, sent_a, wg = turn(chunk_a, partial, other, weight, cotangent, far_cot, dense)
    got_a = send(sent_a, lay.along(True))
    sent_b, kept = rest_terms([chunk_b], back, dense)
    got_b = send(sent_b, lay.along(True))
    got_w1 = send(wg, lay.in_class(2 * near))
    passed_a, kept_a, mark_a = first_sum(chunk_a, got_a, kept, back)
    back_a = send(passed_a, lay.along(False))
    passed_b, kept_b, mark_b = first_sum(chunk_b, got_b, kept, got_w1)
    back_b = send(passed_b, lay.along(False))
    wg = add(wg, got_w1, mark_b)
    got_w2 = send(wg, lay.in_class(near))
    two, three, mark_c = second_sum(back_a, kept_a, jnp.bfloat16, back)
    three = send(three, lay.in_class(3 * near))
    two = send(two, lay.in_class(2 * near))
    zero, one, mark_d = second_sum(back_b, kept_b, jnp.float32, mark_c)
    one = send(one, lay.in_class(near))
    wg = add(wg, got_w2, mark_c)
    wg = add(wg, send(wg, lay.along(True)), mark_d)
    ours = line_sum(three, two, one, zero, wg, send(wg, lay.along(False)))
    feat_grad, weight_grad = finish(ours, send(ours, lay.plain(1, 0)), share)
    return act, feat_grad, weight_grad


def local_any(features, weight, tiles, pos, count, cotangent):
    reps = lax.axis_size("rep")
    lay = Layout(lax.axis_size("blk"), reps)
    r = lax.axis_index("rep")
    sections, tile = tiles.shape[0], tiles.shape[-1]
    rows = features.shape[0]
    blocks, share = rows // tile, rows // reps
    bf = jnp.bfloat16

    line = jnp.concatenate([send(features, lay.owner_to_class(at)) for at in range(sections)], 0)
    dense = dense_blocks(tiles, section_table(pos, count, blocks, 0), 1, 1, blocks)
    size = line.shape[0]
    partial = aggregate(dense, [(0, 0, 0, 0, size)], [line], None, jnp.float32)
    g = lax.psum(partial, "rep").astype(bf)
    value, slope = gelu_and_slope(dot(g, weight))
    cot = lax.all_gather(cotangent, "rep", axis=0, tiled=True)
    grad = (cot.astype(jnp.float32) * slope).astype(bf)
    act = lax.dynamic_slice_in_dim(value, r * share, share, 0).astype(bf)
    own_g = lax.dynamic_slice_in_dim(g, r * share, share, 0)
    own_grad = lax.dynamic_slice_in_dim(grad, r * share, share, 0)
    weight_grad = lax.psum(tn_dot(own_g, own_grad), AXES)
    back = nt_dot(weight, grad).astype(bf)
    terms = dot(back, dense[0]).astype(bf)
    total = jnp.zeros((back.shape[0], rows), jnp.float32)
    for at in range(sections):
        total += send(terms[:, at * rows:(at + 1) * rows], lay.class_to_owner(at)).astype(jnp.float32)
    feat_grad = lax.psum_scatter(total.T, "rep", scatter_dimension=0, tiled=True).astype(bf)
    return act, feat_grad, weight_grad


def local(features, weight, tile_vals, tile_pos, tile_count, cotangent):
    tiles, pos, count = tile_vals[0, 0], tile_pos[0, 0], tile_count[0, 0]
    reps, tile = lax.axis_size("rep"), tiles.shape[-1]
    paired = reps == 2 and tiles.shape[0] == 8 and features.shape[0] % (2 * tile) == 0
    work = local_pairs if paired else local_any
    return work(features, weight, tiles, pos, count, cotangent)


def solution(mesh):
    placed = (
        P("blk", None),
        P(),
        P("blk", "rep", None, None, None, None),
        P("blk", "rep", None, None),
        P("blk", "rep", None),
        P(("blk", "rep"), None),
    )
    return jax.shard_map(
        local,
        mesh=mesh,
        in_specs=placed,
        out_specs=(P(("blk", "rep"), None), P(("blk", "rep"), None), P()),
        check_vma=False,
    )
```

```python
import functools

import jax
import jax.numpy as jnp
from jax import lax
from jax.experimental import pallas as pl
from jax.experimental.pallas import tpu as pltpu
from jax.sharding import PartitionSpec as P

AXES = ("blk", "rep")
VMEM_LIMIT = 16 * 1024 * 1024


def params():
    return pltpu.CompilerParams(vmem_limit_bytes=VMEM_LIMIT)


def in_vmem(count):
    return [pl.BlockSpec(memory_space=pltpu.VMEM)] * count


def held_in_vmem(value):
    return pltpu.with_memory_space_constraint(value, pltpu.VMEM)


def gelu_and_slope(v):
    scale = 0.7978845608028654
    square = v * v
    t = jnp.tanh(scale * (v + 0.044715 * (square * v)))
    half = 0.5 * (1.0 + t)
    slope = half + (0.5 * scale) * v * (1.0 - t * t) * (1.0 + 3.0 * 0.044715 * square)
    return v * half, slope


def nt_dot(a, b):
    return lax.dot_general(a, b, (((1,), (1,)), ((), ())), preferred_element_type=jnp.float32)


def tn_dot(a, b):
    return lax.dot_general(a, b, (((0,), (0,)), ((), ())), preferred_element_type=jnp.float32)


def dot(a, b):
    return jnp.dot(a, b, preferred_element_type=jnp.float32)


def split_by(value, size):
    if size & (size - 1):
        return lax.div(value, size), lax.rem(value, size)
    return lax.shift_right_logical(value, size.bit_length() - 1), value & (size - 1)


def dense_kernel(blocks, near, halves, table, tiles_ref, out_ref, held, arrived):
    sections, slots, tile = held.shape[0], held.shape[1], held.shape[-1]
    piece = out_ref.shape[2] // (sections // near)
    copies = [
        pltpu.make_async_copy(tiles_ref.at[section], held.at[section], arrived.at[section])
        for section in range(sections)
    ]
    for copy in copies:
        copy.start()
    out_ref[...] = jnp.zeros_like(out_ref)
    for section, copy in enumerate(copies):
        copy.wait()
        far_place, near_place = split_by(table[section, slots], near)
        for slot in range(slots):
            cell = table[section, slot]

            @pl.when(cell >= 0)
            def _():
                row, column = split_by(cell, blocks)
                half, column = split_by(column, blocks // halves)
                row_at = pl.multiple_of(row * tile, tile)
                column_at = pl.multiple_of(far_place * piece + column * tile, tile)
                out_ref[near_place * halves + half, pl.ds(row_at, tile), pl.ds(column_at, tile)] = held[section, slot]


def dense_blocks(tiles, table, near, halves, blocks):
    sections, _, tile, _ = tiles.shape
    rows = blocks * tile
    shape = (near * halves, rows, sections // near * rows // halves)
    return pl.pallas_call(
        functools.partial(dense_kernel, blocks, near, halves),
        in_specs=[pl.BlockSpec(memory_space=pltpu.SMEM), pl.BlockSpec(memory_space=pltpu.HBM)],
        out_specs=in_vmem(1)[0],
        out_shape=pltpu.VMEM(shape, jnp.bfloat16),
        scratch_shapes=[pltpu.VMEM(tiles.shape, tiles.dtype), pltpu.SemaphoreType.DMA((sections,))],
        compiler_params=params(),
        name="dense_blocks",
    )(table, pltpu.with_memory_space_constraint(tiles, pltpu.HBM))


def lane_of_class():
    return lax.rem(lax.axis_index("blk") + lax.axis_index("rep"), 2)


def unit_at(unit):
    if unit in (0, 3):
        return unit
    return 2 - lane_of_class() if unit == 1 else 1 + lane_of_class()


def aggregate_kernel(spans, based, dense_ref, *refs):
    given, out_ref = refs[:-1], refs[-1]
    total = given[0][...] if based else None
    halves = 2 if lax.axis_size("rep") == 2 and dense_ref.shape[0] > 1 else 1
    for at, first, start, base, size in spans:
        for half in range(halves):
            row = base if halves == 1 else pl.multiple_of(base + (half ^ lax.axis_index("rep")) * size, size)
            term = dot(dense_ref[first + half, :, pl.ds(start, size)], given[based + at][pl.ds(row, size), :])
            total = term if total is None else total + term
    out_ref[...] = total.astype(out_ref.dtype)


def aggregate(dense, spans, parts, base, dtype):
    rows, width = dense.shape[1], parts[0].shape[1]
    given = ([] if base is None else [base]) + parts
    return pl.pallas_call(
        functools.partial(aggregate_kernel, spans, len(given) - len(parts)),
        in_specs=in_vmem(1 + len(given)),
        out_specs=in_vmem(1)[0],
        out_shape=jax.ShapeDtypeStruct((rows, width), dtype),
        compiler_params=params(),
        name="aggregate",
    )(held_in_vmem(dense), *given)


def turn_kernel(share, chunk, own_ref, other_ref, weight_ref, cot_ref, far_cot_ref, dense_ref,
                act_ref, back_ref, sent_ref, g_ref, grad_ref):
    rows = own_ref.shape[0]
    weight = weight_ref[...]
    for half, cot in enumerate((cot_ref, far_cot_ref)):
        at, there = half * share, rows - share - half * share
        g = own_ref[pl.ds(at, share), :].astype(jnp.float32) + other_ref[pl.ds(there, share), :].astype(jnp.float32)
        g = g.astype(jnp.bfloat16)
        value, slope = gelu_and_slope(dot(g, weight))
        grad = (cot[...].astype(jnp.float32) * slope).astype(jnp.bfloat16)
        if half == 0:
            act_ref[...] = value.astype(jnp.bfloat16)
        g_ref[pl.ds(at, share), :] = g
        grad_ref[pl.ds(at, share), :] = grad
        back_ref[:, pl.ds(at, share)] = nt_dot(weight, grad).astype(jnp.bfloat16)
    back = back_ref[...]
    start, size = chunk
    for second in range(2):
        term = dot(back, dense_ref[unit_at(2 + second), :, pl.ds(start, size)])
        sent_ref[:, pl.ds(second * size, size)] = term.astype(jnp.bfloat16)


def turn(chunk, own, other, weight, cot, far_cot, dense):
    rows, width = own.shape
    share, hid = cot.shape
    bf = jnp.bfloat16
    return pl.pallas_call(
        functools.partial(turn_kernel, share, chunk),
        in_specs=in_vmem(6),
        out_specs=in_vmem(5),
        out_shape=[
            pltpu.VMEM((share, hid), bf),
            jax.ShapeDtypeStruct((width, rows), bf),
            jax.ShapeDtypeStruct((width, 2 * chunk[1]), bf),
            jax.ShapeDtypeStruct((rows, width), bf),
            jax.ShapeDtypeStruct((rows, hid), bf),
        ],
        compiler_params=params(),
        name="turn",
    )(own, other, weight, cot, far_cot, held_in_vmem(dense))


def rest_kernel(chunks, back_ref, dense_ref, g_ref, grad_ref, wg_ref, *refs):
    back = back_ref[...]
    for (start, size), sent in zip(chunks, refs[:-1]):
        for second in range(2):
            term = dot(back, dense_ref[unit_at(2 + second), :, pl.ds(start, size)])
            sent[:, pl.ds(second * size, size)] = term.astype(jnp.bfloat16)
    part = wg_ref.shape[1]
    columns = pl.ds(pl.multiple_of(lane_of_class() * part, part), part)
    wg_ref[...] = tn_dot(g_ref[...], grad_ref[:, columns]).astype(jnp.bfloat16)
    for second in range(2):
        refs[-1][second] = dot(back, dense_ref[unit_at(second)])


def rest_terms(chunks, back, dense, g, grad):
    width, span = back.shape[0], dense.shape[2]
    return pl.pallas_call(
        functools.partial(rest_kernel, chunks),
        in_specs=in_vmem(4),
        out_specs=in_vmem(len(chunks) + 2),
        out_shape=[jax.ShapeDtypeStruct((width, grad.shape[1] // 2), jnp.bfloat16)]
        + [jax.ShapeDtypeStruct((width, 2 * size), jnp.bfloat16) for _, size in chunks]
        + [jax.ShapeDtypeStruct((2, width, span), jnp.float32)],
        compiler_params=params(),
        name="rest_terms",
    )(back, held_in_vmem(dense), g, grad)


def first_sum_kernel(start, size, got_ref, kept_ref, after_ref, sent_ref, total_ref, mark_ref):
    total_ref[...] = kept_ref[0, :, pl.ds(start, size)] + got_ref[:, pl.ds(0, size)].astype(jnp.float32)
    passed = kept_ref[1, :, pl.ds(start, size)] + got_ref[:, pl.ds(size, size)].astype(jnp.float32)
    sent_ref[...] = passed.astype(jnp.bfloat16)
    mark_ref[...] = jnp.zeros_like(mark_ref)


MARK = jax.ShapeDtypeStruct((16, 128), jnp.bfloat16)


def first_sum(chunk, got, kept, after):
    width = kept.shape[1]
    start, size = chunk
    return pl.pallas_call(
        functools.partial(first_sum_kernel, start, size),
        in_specs=in_vmem(3),
        out_specs=in_vmem(3),
        out_shape=[
            jax.ShapeDtypeStruct((width, size), jnp.bfloat16),
            jax.ShapeDtypeStruct((width, size), jnp.float32),
            MARK,
        ],
        compiler_params=params(),
        name="first_sum",
    )(got, kept, after)


def second_sum_kernel(got_ref, kept_ref, after_ref, first_ref, second_ref, mark_ref):
    piece = kept_ref.shape[1] // 2
    for at, out in enumerate((first_ref, second_ref)):
        span = pl.ds(at * piece, piece)
        out[...] = (kept_ref[:, span] + got_ref[:, span].astype(jnp.float32)).astype(out.dtype)
    mark_ref[...] = jnp.zeros_like(mark_ref)


def second_sum(got, kept, first_type, after):
    width, size = kept.shape
    return pl.pallas_call(
        second_sum_kernel,
        in_specs=in_vmem(3),
        out_specs=in_vmem(3),
        out_shape=[jax.ShapeDtypeStruct((width, size // 2), kind) for kind in (first_type, jnp.bfloat16)] + [MARK],
        compiler_params=params(),
        name="second_sum",
    )(got, kept, after)


def add_kernel(a_ref, b_ref, after_ref, out_ref):
    out_ref[...] = (a_ref[...].astype(jnp.float32) + b_ref[...].astype(jnp.float32)).astype(out_ref.dtype)


def add(a, b, after):
    return pl.pallas_call(
        add_kernel,
        in_specs=in_vmem(3),
        out_specs=in_vmem(1)[0],
        out_shape=jax.ShapeDtypeStruct(a.shape, a.dtype),
        compiler_params=params(),
        name="add",
    )(a, b, after)


def line_sum_kernel(three_ref, two_ref, one_ref, zero_ref, wg_ref, got_wg_ref, out_ref):
    piece = zero_ref.shape[1]
    span, tail = pl.ds(0, piece), pl.ds(piece, out_ref.shape[1] - piece)
    three, two, one = [ref[...].astype(jnp.float32) for ref in (three_ref, two_ref, one_ref)]
    out_ref[:, span] = ((zero_ref[...] + one) + (two + three)).astype(jnp.bfloat16)
    out_ref[:, tail] = (wg_ref[...].astype(jnp.float32) + got_wg_ref[...].astype(jnp.float32)).astype(jnp.bfloat16)


def line_sum(three, two, one, zero, wg, got_wg):
    width, piece = zero.shape
    return pl.pallas_call(
        line_sum_kernel,
        in_specs=in_vmem(6),
        out_specs=in_vmem(1)[0],
        out_shape=jax.ShapeDtypeStruct((width, piece + wg.shape[1]), jnp.bfloat16),
        compiler_params=params(),
        name="line_sum",
    )(three, two, one, zero, wg, got_wg)


def finish_kernel(own_ref, got_ref, feat_ref, wg_ref):
    piece = feat_ref.shape[0]
    part = own_ref.shape[1] - piece
    lane = lane_of_class()
    wg_ref[:, pl.ds(pl.multiple_of(lane * part, part), part)] = own_ref[:, pl.ds(piece, part)].astype(jnp.float32)
    wg_ref[:, pl.ds(pl.multiple_of((1 - lane) * part, part), part)] = got_ref[:, pl.ds(piece, part)].astype(jnp.float32)
    span = pl.ds(0, piece)
    ours = jnp.where(lax.axis_index("rep") == 0, own_ref[:, span].astype(jnp.float32), got_ref[:, span].astype(jnp.float32))
    feat_ref[...] = ours.T.astype(jnp.bfloat16)


def finish(own, got, piece):
    width, total = own.shape
    return pl.pallas_call(
        finish_kernel,
        in_specs=in_vmem(2),
        out_specs=in_vmem(2),
        out_shape=[
            jax.ShapeDtypeStruct((piece, width), jnp.bfloat16),
            jax.ShapeDtypeStruct((width, 2 * (total - piece)), jnp.float32),
        ],
        compiler_params=params(),
        name="finish",
    )(own, got)


class Layout:
    def __init__(self, n_blk, reps):
        self.n_blk, self.reps = n_blk, reps

    def route(self, moved):
        pairs = []
        for b in range(self.n_blk):
            for r in range(self.reps):
                to_b, to_r = moved(b, r)
                pairs.append((b * self.reps + r, to_b * self.reps + to_r))
        return pairs

    def owner_to_class(self, mask):
        reps = self.reps
        return self.route(lambda b, r: (((b // reps) ^ mask) * reps + (b + r) % reps, r))

    def class_to_owner(self, mask):
        reps = self.reps
        return self.route(lambda b, r: (((b // reps) ^ mask) * reps + (b - r) % reps, r))

    def in_class(self, mask):
        return self.route(lambda b, r: (b ^ (mask * self.reps), r))

    def along(self, first):
        reps = self.reps

        def moved(b, r):
            lane = (b - r) % reps
            mask, rep_mask = (0, 1) if (lane == 0) == first else (1, 0)
            to_r = r ^ rep_mask
            return (((b // reps) ^ mask) * reps + (lane + to_r) % reps, to_r)

        return self.route(moved)

    def plain(self, mask, rep_mask):
        return self.route(lambda b, r: (b ^ mask, r ^ rep_mask))


def send(value, route):
    return lax.ppermute(value, AXES, route)


def section_table(pos, count, blocks, flip):
    reps, n_blk = lax.axis_size("rep"), lax.axis_size("blk")
    b, r = lax.axis_index("blk"), lax.axis_index("rep")
    sections, slots = pos.shape
    columns = (b - r - jnp.arange(sections, dtype=jnp.int32) * reps) % n_blk
    places = (columns // reps) ^ (b // reps)
    live = jnp.arange(slots, dtype=jnp.int32)[None, :] < count[:, None]
    cells = jnp.where(live, pos ^ (flip * (blocks + 1)), -1)
    return jnp.concatenate([cells, places[:, None]], 1).astype(jnp.int32)


def local_pairs(features, weight, tiles, pos, count, cotangent):
    near, halves = 2, 2
    lay = Layout(lax.axis_size("blk"), lax.axis_size("rep"))
    b, r = lax.axis_index("blk"), lax.axis_index("rep")
    sections, tile = tiles.shape[0], tiles.shape[-1]
    rows, width = features.shape
    blocks, share = rows // tile, rows // halves
    table = section_table(pos, count, blocks, r * (blocks // halves))
    two, one = [send(features, lay.owner_to_class(at * near)) for at in (2, 1)]
    whole, whole_beside = [send(features, lay.owner_to_class(at)) for at in range(2)]
    far_cot = send(cotangent, lay.plain(0, 1))
    three = send(two, lay.in_class(near))
    mine = jnp.concatenate([two, one], 0)
    beside = send(mine, lay.in_class(1))
    beside_three = send(three, lay.in_class(1))
    dense = dense_blocks(tiles, table, near, halves, blocks)
    spans = [(0, 0, 0, 0, share), (1, 2, 0, 0, share), (2, 0, 2 * share, 0, share), (2, 0, share, rows, share),
             (3, 2, 2 * share, 0, share), (3, 2, share, rows, share), (4, 0, 3 * share, 0, share)]
    partial = aggregate(dense, spans, [whole, whole_beside, mine, beside, three], None, jnp.float32)
    partial = aggregate(dense, [(0, 2, 3 * share, 0, share)], [beside_three], partial, jnp.bfloat16)
    other = send(partial, lay.plain(0, 1))
    chunk_a, chunk_b = (2 * share, 2 * share), (0, 2 * share)
    act, back, sent_a, g, grad = turn(chunk_a, partial, other, weight, cotangent, far_cot, dense)
    got_a = send(sent_a, lay.along(True))
    wg, sent_b, kept = rest_terms([chunk_b], back, dense, g, grad)
    got_b = send(sent_b, lay.along(True))
    got_w1 = send(wg, lay.in_class(2 * near))
    passed_a, kept_a, mark_a = first_sum(chunk_a, got_a, kept, back)
    back_a = send(passed_a, lay.along(False))
    passed_b, kept_b, mark_b = first_sum(chunk_b, got_b, kept, got_w1)
    back_b = send(passed_b, lay.along(False))
    wg = add(wg, got_w1, mark_b)
    got_w2 = send(wg, lay.in_class(near))
    two, three, mark_c = second_sum(back_a, kept_a, jnp.bfloat16, back)
    three = send(three, lay.in_class(3 * near))
    two = send(two, lay.in_class(2 * near))
    zero, one, mark_d = second_sum(back_b, kept_b, jnp.float32, mark_c)
    one = send(one, lay.in_class(near))
    wg = add(wg, got_w2, mark_c)
    wg = add(wg, send(wg, lay.along(True)), mark_d)
    ours = line_sum(three, two, one, zero, wg, send(wg, lay.along(False)))
    feat_grad, weight_grad = finish(ours, send(ours, lay.plain(1, 0)), share)
    return act, feat_grad, weight_grad


def local_any(features, weight, tiles, pos, count, cotangent):
    reps = lax.axis_size("rep")
    lay = Layout(lax.axis_size("blk"), reps)
    r = lax.axis_index("rep")
    sections, tile = tiles.shape[0], tiles.shape[-1]
    rows = features.shape[0]
    blocks, share = rows // tile, rows // reps
    bf = jnp.bfloat16

    line = jnp.concatenate([send(features, lay.owner_to_class(at)) for at in range(sections)], 0)
    dense = dense_blocks(tiles, section_table(pos, count, blocks, 0), 1, 1, blocks)
    size = line.shape[0]
    partial = aggregate(dense, [(0, 0, 0, 0, size)], [line], None, jnp.float32)
    g = lax.psum(partial, "rep").astype(bf)
    value, slope = gelu_and_slope(dot(g, weight))
    cot = lax.all_gather(cotangent, "rep", axis=0, tiled=True)
    grad = (cot.astype(jnp.float32) * slope).astype(bf)
    act = lax.dynamic_slice_in_dim(value, r * share, share, 0).astype(bf)
    own_g = lax.dynamic_slice_in_dim(g, r * share, share, 0)
    own_grad = lax.dynamic_slice_in_dim(grad, r * share, share, 0)
    weight_grad = lax.psum(tn_dot(own_g, own_grad), AXES)
    back = nt_dot(weight, grad).astype(bf)
    terms = dot(back, dense[0]).astype(bf)
    total = jnp.zeros((back.shape[0], rows), jnp.float32)
    for at in range(sections):
        total += send(terms[:, at * rows:(at + 1) * rows], lay.class_to_owner(at)).astype(jnp.float32)
    feat_grad = lax.psum_scatter(total.T, "rep", scatter_dimension=0, tiled=True).astype(bf)
    return act, feat_grad, weight_grad


def local(features, weight, tile_vals, tile_pos, tile_count, cotangent):
    tiles, pos, count = tile_vals[0, 0], tile_pos[0, 0], tile_count[0, 0]
    reps, tile = lax.axis_size("rep"), tiles.shape[-1]
    paired = reps == 2 and tiles.shape[0] == 8 and features.shape[0] % (2 * tile) == 0
    work = local_pairs if paired else local_any
    return work(features, weight, tiles, pos, count, cotangent)


def solution(mesh):
    placed = (
        P("blk", None),
        P(),
        P("blk", "rep", None, None, None, None),
        P("blk", "rep", None, None),
        P("blk", "rep", None),
        P(("blk", "rep"), None),
    )
    return jax.shard_map(
        local,
        mesh=mesh,
        in_specs=placed,
        out_specs=(P(("blk", "rep"), None), P(("blk", "rep"), None), P()),
        check_vma=False,
    )
```

```python
import functools

import jax
import jax.numpy as jnp
from jax import lax
from jax.experimental import pallas as pl
from jax.experimental.pallas import tpu as pltpu
from jax.sharding import PartitionSpec as P

AXES = ("blk", "rep")
VMEM_LIMIT = 16 * 1024 * 1024


def params():
    return pltpu.CompilerParams(vmem_limit_bytes=VMEM_LIMIT)


def in_vmem(count):
    return [pl.BlockSpec(memory_space=pltpu.VMEM)] * count


def held_in_vmem(value):
    return pltpu.with_memory_space_constraint(value, pltpu.VMEM)


def gelu_and_slope(v):
    scale = 0.7978845608028654
    square = v * v
    t = jnp.tanh(scale * (v + 0.044715 * (square * v)))
    half = 0.5 * (1.0 + t)
    slope = half + (0.5 * scale) * v * (1.0 - t * t) * (1.0 + 3.0 * 0.044715 * square)
    return v * half, slope


def nt_dot(a, b):
    return lax.dot_general(a, b, (((1,), (1,)), ((), ())), preferred_element_type=jnp.float32)


def tn_dot(a, b):
    return lax.dot_general(a, b, (((0,), (0,)), ((), ())), preferred_element_type=jnp.float32)


def dot(a, b):
    return jnp.dot(a, b, preferred_element_type=jnp.float32)


def split_by(value, size):
    if size & (size - 1):
        return lax.div(value, size), lax.rem(value, size)
    return lax.shift_right_logical(value, size.bit_length() - 1), value & (size - 1)


def dense_kernel(blocks, near, halves, table, tiles_ref, out_ref, held, arrived):
    sections, slots, tile = held.shape[0], held.shape[1], held.shape[-1]
    piece = out_ref.shape[2] // (sections // near)
    copies = [
        pltpu.make_async_copy(tiles_ref.at[section], held.at[section], arrived.at[section])
        for section in range(sections)
    ]
    for copy in copies:
        copy.start()
    out_ref[...] = jnp.zeros_like(out_ref)
    for section, copy in enumerate(copies):
        copy.wait()
        far_place, near_place = split_by(table[section, slots], near)
        for slot in range(slots):
            cell = table[section, slot]

            @pl.when(cell >= 0)
            def _():
                row, column = split_by(cell, blocks)
                half, column = split_by(column, blocks // halves)
                row_at = pl.multiple_of(row * tile, tile)
                column_at = pl.multiple_of(far_place * piece + column * tile, tile)
                out_ref[near_place * halves + half, pl.ds(row_at, tile), pl.ds(column_at, tile)] = held[section, slot]


def dense_blocks(tiles, table, near, halves, blocks):
    sections, _, tile, _ = tiles.shape
    rows = blocks * tile
    shape = (near * halves, rows, sections // near * rows // halves)
    return pl.pallas_call(
        functools.partial(dense_kernel, blocks, near, halves),
        in_specs=[pl.BlockSpec(memory_space=pltpu.SMEM), pl.BlockSpec(memory_space=pltpu.HBM)],
        out_specs=in_vmem(1)[0],
        out_shape=pltpu.VMEM(shape, jnp.bfloat16),
        scratch_shapes=[pltpu.VMEM(tiles.shape, tiles.dtype), pltpu.SemaphoreType.DMA((sections,))],
        compiler_params=params(),
        name="dense_blocks",
    )(table, pltpu.with_memory_space_constraint(tiles, pltpu.HBM))


def lane_of_class():
    return lax.rem(lax.axis_index("blk") + lax.axis_index("rep"), 2)


def unit_at(unit):
    if unit in (0, 3):
        return unit
    return 2 - lane_of_class() if unit == 1 else 1 + lane_of_class()


def aggregate_kernel(spans, based, dense_ref, *refs):
    given, out_ref = refs[:-1], refs[-1]
    total = given[0][...] if based else None
    halves = 2 if lax.axis_size("rep") == 2 and dense_ref.shape[0] > 1 else 1
    for at, first, start, base, size in spans:
        for half in range(halves):
            row = base if halves == 1 else pl.multiple_of(base + (half ^ lax.axis_index("rep")) * size, size)
            term = dot(dense_ref[first + half, :, pl.ds(start, size)], given[based + at][pl.ds(row, size), :])
            total = term if total is None else total + term
    out_ref[...] = total.astype(out_ref.dtype)


def aggregate(dense, spans, parts, base, dtype):
    rows, width = dense.shape[1], parts[0].shape[1]
    given = ([] if base is None else [base]) + parts
    return pl.pallas_call(
        functools.partial(aggregate_kernel, spans, len(given) - len(parts)),
        in_specs=in_vmem(1 + len(given)),
        out_specs=in_vmem(1)[0],
        out_shape=jax.ShapeDtypeStruct((rows, width), dtype),
        compiler_params=params(),
        name="aggregate",
    )(held_in_vmem(dense), *given)


def turn_kernel(share, chunk, own_ref, other_ref, weight_ref, cot_ref, far_cot_ref, dense_ref,
                act_ref, back_ref, sent_ref, g_ref, grad_ref):
    rows = own_ref.shape[0]
    weight = weight_ref[...]
    for half, cot in enumerate((cot_ref, far_cot_ref)):
        at, there = half * share, rows - share - half * share
        g = own_ref[pl.ds(at, share), :].astype(jnp.float32) + other_ref[pl.ds(there, share), :].astype(jnp.float32)
        g = g.astype(jnp.bfloat16)
        value, slope = gelu_and_slope(dot(g, weight))
        grad = (cot[...].astype(jnp.float32) * slope).astype(jnp.bfloat16)
        if half == 0:
            act_ref[...] = value.astype(jnp.bfloat16)
        g_ref[pl.ds(at, share), :] = g
        grad_ref[pl.ds(at, share), :] = grad
        back_ref[:, pl.ds(at, share)] = nt_dot(weight, grad).astype(jnp.bfloat16)
    back = back_ref[...]
    start, size = chunk
    for second in range(2):
        term = dot(back, dense_ref[unit_at(2 + second), :, pl.ds(start, size)])
        sent_ref[:, pl.ds(second * size, size)] = term.astype(jnp.bfloat16)


def turn(chunk, own, other, weight, cot, far_cot, dense):
    rows, width = own.shape
    share, hid = cot.shape
    bf = jnp.bfloat16
    return pl.pallas_call(
        functools.partial(turn_kernel, share, chunk),
        in_specs=in_vmem(6),
        out_specs=in_vmem(5),
        out_shape=[
            pltpu.VMEM((share, hid), bf),
            jax.ShapeDtypeStruct((width, rows), bf),
            jax.ShapeDtypeStruct((width, 2 * chunk[1]), bf),
            jax.ShapeDtypeStruct((rows, width), bf),
            jax.ShapeDtypeStruct((rows, hid), bf),
        ],
        compiler_params=params(),
        name="turn",
    )(own, other, weight, cot, far_cot, held_in_vmem(dense))


def rest_kernel(chunks, back_ref, dense_ref, g_ref, grad_ref, wg_ref, *refs):
    back = back_ref[...]
    for (start, size), sent in zip(chunks, refs[:-1]):
        for second in range(2):
            term = dot(back, dense_ref[unit_at(2 + second), :, pl.ds(start, size)])
            sent[:, pl.ds(second * size, size)] = term.astype(jnp.bfloat16)
    part = wg_ref.shape[1]
    columns = pl.ds(pl.multiple_of(lane_of_class() * part, part), part)
    wg_ref[...] = tn_dot(g_ref[...], grad_ref[:, columns]).astype(jnp.bfloat16)
    for second in range(2):
        refs[-1][second] = dot(back, dense_ref[unit_at(second)])


def rest_terms(chunks, back, dense, g, grad):
    width, span = back.shape[0], dense.shape[2]
    return pl.pallas_call(
        functools.partial(rest_kernel, chunks),
        in_specs=in_vmem(4),
        out_specs=in_vmem(len(chunks) + 2),
        out_shape=[jax.ShapeDtypeStruct((width, grad.shape[1] // 2), jnp.bfloat16)]
        + [jax.ShapeDtypeStruct((width, 2 * size), jnp.bfloat16) for _, size in chunks]
        + [jax.ShapeDtypeStruct((2, width, span), jnp.float32)],
        compiler_params=params(),
        name="rest_terms",
    )(back, held_in_vmem(dense), g, grad)


def first_sum_kernel(start, size, got_ref, kept_ref, after_ref, sent_ref, total_ref, mark_ref):
    total_ref[...] = kept_ref[0, :, pl.ds(start, size)] + got_ref[:, pl.ds(0, size)].astype(jnp.float32)
    passed = kept_ref[1, :, pl.ds(start, size)] + got_ref[:, pl.ds(size, size)].astype(jnp.float32)
    sent_ref[...] = passed.astype(jnp.bfloat16)
    mark_ref[...] = jnp.zeros_like(mark_ref)


MARK = jax.ShapeDtypeStruct((16, 128), jnp.bfloat16)


def first_sum(chunk, got, kept, after):
    width = kept.shape[1]
    start, size = chunk
    return pl.pallas_call(
        functools.partial(first_sum_kernel, start, size),
        in_specs=in_vmem(3),
        out_specs=in_vmem(3),
        out_shape=[
            jax.ShapeDtypeStruct((width, size), jnp.bfloat16),
            jax.ShapeDtypeStruct((width, size), jnp.float32),
            MARK,
        ],
        compiler_params=params(),
        name="first_sum",
    )(got, kept, after)


def second_sum_kernel(got_ref, kept_ref, after_ref, first_ref, second_ref, mark_ref):
    piece = kept_ref.shape[1] // 2
    for at, out in enumerate((first_ref, second_ref)):
        span = pl.ds(at * piece, piece)
        out[...] = (kept_ref[:, span] + got_ref[:, span].astype(jnp.float32)).astype(out.dtype)
    mark_ref[...] = jnp.zeros_like(mark_ref)


def second_sum(got, kept, first_type, after):
    width, size = kept.shape
    return pl.pallas_call(
        second_sum_kernel,
        in_specs=in_vmem(3),
        out_specs=in_vmem(3),
        out_shape=[jax.ShapeDtypeStruct((width, size // 2), kind) for kind in (first_type, jnp.bfloat16)] + [MARK],
        compiler_params=params(),
        name="second_sum",
    )(got, kept, after)


def add_kernel(a_ref, b_ref, after_ref, out_ref):
    out_ref[...] = (a_ref[...].astype(jnp.float32) + b_ref[...].astype(jnp.float32)).astype(out_ref.dtype)


def add(a, b, after):
    return pl.pallas_call(
        add_kernel,
        in_specs=in_vmem(3),
        out_specs=in_vmem(1)[0],
        out_shape=jax.ShapeDtypeStruct(a.shape, a.dtype),
        compiler_params=params(),
        name="add",
    )(a, b, after)


def line_sum_kernel(three_ref, two_ref, one_ref, zero_ref, wg_ref, got_wg_ref, out_ref):
    piece = zero_ref.shape[1]
    span, tail = pl.ds(0, piece), pl.ds(piece, out_ref.shape[1] - piece)
    three, two, one = [ref[...].astype(jnp.float32) for ref in (three_ref, two_ref, one_ref)]
    out_ref[:, span] = ((zero_ref[...] + one) + (two + three)).astype(jnp.bfloat16)
    out_ref[:, tail] = (wg_ref[...].astype(jnp.float32) + got_wg_ref[...].astype(jnp.float32)).astype(jnp.bfloat16)


def line_sum(three, two, one, zero, wg, got_wg):
    width, piece = zero.shape
    return pl.pallas_call(
        line_sum_kernel,
        in_specs=in_vmem(6),
        out_specs=in_vmem(1)[0],
        out_shape=jax.ShapeDtypeStruct((width, piece + wg.shape[1]), jnp.bfloat16),
        compiler_params=params(),
        name="line_sum",
    )(three, two, one, zero, wg, got_wg)


def finish_kernel(own_ref, got_ref, feat_ref, wg_ref):
    piece = feat_ref.shape[0]
    part = own_ref.shape[1] - piece
    lane = lane_of_class()
    wg_ref[:, pl.ds(pl.multiple_of(lane * part, part), part)] = own_ref[:, pl.ds(piece, part)].astype(jnp.float32)
    wg_ref[:, pl.ds(pl.multiple_of((1 - lane) * part, part), part)] = got_ref[:, pl.ds(piece, part)].astype(jnp.float32)
    span = pl.ds(0, piece)
    ours = jnp.where(lax.axis_index("rep") == 0, own_ref[:, span].astype(jnp.float32), got_ref[:, span].astype(jnp.float32))
    feat_ref[...] = ours.T.astype(jnp.bfloat16)


def finish(own, got, piece):
    width, total = own.shape
    return pl.pallas_call(
        finish_kernel,
        in_specs=in_vmem(2),
        out_specs=in_vmem(2),
        out_shape=[
            jax.ShapeDtypeStruct((piece, width), jnp.bfloat16),
            jax.ShapeDtypeStruct((width, 2 * (total - piece)), jnp.float32),
        ],
        compiler_params=params(),
        name="finish",
    )(own, got)


class Layout:
    def __init__(self, n_blk, reps):
        self.n_blk, self.reps = n_blk, reps

    def route(self, moved):
        pairs = []
        for b in range(self.n_blk):
            for r in range(self.reps):
                to_b, to_r = moved(b, r)
                pairs.append((b * self.reps + r, to_b * self.reps + to_r))
        return pairs

    def owner_to_class(self, mask):
        reps = self.reps
        return self.route(lambda b, r: (((b // reps) ^ mask) * reps + (b + r) % reps, r))

    def class_to_owner(self, mask):
        reps = self.reps
        return self.route(lambda b, r: (((b // reps) ^ mask) * reps + (b - r) % reps, r))

    def in_class(self, mask):
        return self.route(lambda b, r: (b ^ (mask * self.reps), r))

    def along(self, first):
        reps = self.reps

        def moved(b, r):
            lane = (b - r) % reps
            mask, rep_mask = (0, 1) if (lane == 0) == first else (1, 0)
            to_r = r ^ rep_mask
            return (((b // reps) ^ mask) * reps + (lane + to_r) % reps, to_r)

        return self.route(moved)

    def plain(self, mask, rep_mask):
        return self.route(lambda b, r: (b ^ mask, r ^ rep_mask))


def send(value, route):
    return lax.ppermute(value, AXES, route)


def section_table(pos, count, blocks, flip):
    reps, n_blk = lax.axis_size("rep"), lax.axis_size("blk")
    b, r = lax.axis_index("blk"), lax.axis_index("rep")
    sections, slots = pos.shape
    columns = (b - r - jnp.arange(sections, dtype=jnp.int32) * reps) % n_blk
    places = (columns // reps) ^ (b // reps)
    live = jnp.arange(slots, dtype=jnp.int32)[None, :] < count[:, None]
    cells = jnp.where(live, pos ^ (flip * (blocks + 1)), -1)
    return jnp.concatenate([cells, places[:, None]], 1).astype(jnp.int32)


def local_pairs(features, weight, tiles, pos, count, cotangent):
    near, halves = 2, 2
    lay = Layout(lax.axis_size("blk"), lax.axis_size("rep"))
    b, r = lax.axis_index("blk"), lax.axis_index("rep")
    sections, tile = tiles.shape[0], tiles.shape[-1]
    rows, width = features.shape
    blocks, share = rows // tile, rows // halves
    table = section_table(pos, count, blocks, r * (blocks // halves))
    two, one = [send(features, lay.owner_to_class(at * near)) for at in (2, 1)]
    whole, whole_beside = [send(features, lay.owner_to_class(at)) for at in range(2)]
    far_cot = send(cotangent, lay.plain(0, 1))
    three = send(two, lay.in_class(near))
    mine = jnp.concatenate([two, one], 0)
    beside = send(mine, lay.in_class(1))
    beside_three = send(three, lay.in_class(1))
    dense = dense_blocks(tiles, table, near, halves, blocks)
    spans = [(0, 0, 0, 0, share), (1, 2, 0, 0, share), (2, 0, 2 * share, 0, share), (2, 0, share, rows, share),
             (3, 2, 2 * share, 0, share), (3, 2, share, rows, share), (4, 0, 3 * share, 0, share)]
    partial = aggregate(dense, spans, [whole, whole_beside, mine, beside, three], None, jnp.float32)
    partial = aggregate(dense, [(0, 2, 3 * share, 0, share)], [beside_three], partial, jnp.bfloat16)
    other = send(partial, lay.plain(0, 1))
    chunk_a, chunk_b = (2 * share, 2 * share), (0, 2 * share)
    act, back, sent_a, g, grad = turn(chunk_a, partial, other, weight, cotangent, far_cot, dense)
    got_a = send(sent_a, lay.along(True))
    wg, sent_b, kept = rest_terms([chunk_b], back, dense, g, grad)
    got_b = send(sent_b, lay.along(True))
    got_w1 = send(wg, lay.in_class(2 * near))
    passed_a, kept_a, mark_a = first_sum(chunk_a, got_a, kept, back)
    back_a = send(passed_a, lay.along(False))
    passed_b, kept_b, mark_b = first_sum(chunk_b, got_b, kept, got_w1)
    back_b = send(passed_b, lay.along(False))
    wg = add(wg, got_w1, mark_b)
    got_w2 = send(wg, lay.in_class(near))
    two, three, mark_c = second_sum(back_a, kept_a, jnp.bfloat16, mark_a)
    three = send(three, lay.in_class(3 * near))
    two = send(two, lay.in_class(2 * near))
    zero, one, mark_d = second_sum(back_b, kept_b, jnp.float32, mark_c)
    one = send(one, lay.in_class(near))
    wg = add(wg, got_w2, mark_c)
    wg = add(wg, send(wg, lay.along(True)), mark_d)
    ours = line_sum(three, two, one, zero, wg, send(wg, lay.along(False)))
    feat_grad, weight_grad = finish(ours, send(ours, lay.plain(1, 0)), share)
    return act, feat_grad, weight_grad


def local_any(features, weight, tiles, pos, count, cotangent):
    reps = lax.axis_size("rep")
    lay = Layout(lax.axis_size("blk"), reps)
    r = lax.axis_index("rep")
    sections, tile = tiles.shape[0], tiles.shape[-1]
    rows = features.shape[0]
    blocks, share = rows // tile, rows // reps
    bf = jnp.bfloat16

    line = jnp.concatenate([send(features, lay.owner_to_class(at)) for at in range(sections)], 0)
    dense = dense_blocks(tiles, section_table(pos, count, blocks, 0), 1, 1, blocks)
    size = line.shape[0]
    partial = aggregate(dense, [(0, 0, 0, 0, size)], [line], None, jnp.float32)
    g = lax.psum(partial, "rep").astype(bf)
    value, slope = gelu_and_slope(dot(g, weight))
    cot = lax.all_gather(cotangent, "rep", axis=0, tiled=True)
    grad = (cot.astype(jnp.float32) * slope).astype(bf)
    act = lax.dynamic_slice_in_dim(value, r * share, share, 0).astype(bf)
    own_g = lax.dynamic_slice_in_dim(g, r * share, share, 0)
    own_grad = lax.dynamic_slice_in_dim(grad, r * share, share, 0)
    weight_grad = lax.psum(tn_dot(own_g, own_grad), AXES)
    back = nt_dot(weight, grad).astype(bf)
    terms = dot(back, dense[0]).astype(bf)
    total = jnp.zeros((back.shape[0], rows), jnp.float32)
    for at in range(sections):
        total += send(terms[:, at * rows:(at + 1) * rows], lay.class_to_owner(at)).astype(jnp.float32)
    feat_grad = lax.psum_scatter(total.T, "rep", scatter_dimension=0, tiled=True).astype(bf)
    return act, feat_grad, weight_grad


def local(features, weight, tile_vals, tile_pos, tile_count, cotangent):
    tiles, pos, count = tile_vals[0, 0], tile_pos[0, 0], tile_count[0, 0]
    reps, tile = lax.axis_size("rep"), tiles.shape[-1]
    paired = reps == 2 and tiles.shape[0] == 8 and features.shape[0] % (2 * tile) == 0
    work = local_pairs if paired else local_any
    return work(features, weight, tiles, pos, count, cotangent)


def solution(mesh):
    placed = (
        P("blk", None),
        P(),
        P("blk", "rep", None, None, None, None),
        P("blk", "rep", None, None),
        P("blk", "rep", None),
        P(("blk", "rep"), None),
    )
    return jax.shard_map(
        local,
        mesh=mesh,
        in_specs=placed,
        out_specs=(P(("blk", "rep"), None), P(("blk", "rep"), None), P()),
        check_vma=False,
    )
```
